512 devices in a mesh: group: 16 (over z), replica: 32 (over y, x, core).
Axes of the slice: x: 4, y: 4, z: 16, core: 2. Of those that a mesh axis runs over, the one named last changes fastest.
Arguments:
- gradient: bfloat16 [512, 32, 20480], P(('group', 'replica')), may hold values from -24 to 24
- residual: bfloat16 [512, 32, 20480], P(('group', 'replica')), may hold values from -4 to 4
- q_prev: float32 [20480, 16], P(('group', 'replica')), may hold values from -6 to 6
- p_bits: int32 [512, 32, 16], P(('group', 'replica')), may hold values from 0 to 2097151
- q_bits: int32 [512, 20480, 8], P(('group', 'replica')), may hold values from 0 to 8191
Outputs:
- q_next: float32 [20480, 16], P(('group', 'replica'))
- new_residual: bfloat16 [512, 32, 20480], P(('group', 'replica'))
The draws below stay inside these ranges and needn't reach their ends.
All inputs are finite; a program needn't handle non-finite values.
Results may differ from the reference program's by a relative error of at most 0.012.
Values sent between devices are 32-bit elements; how exact they have to be, the bound alone decides.
No kernel may reach another device: no remote copies, remote signals or barrier semaphores. Data moves between devices by JAX's collectives and lax.ppermute only.
A program may use at most 64 MiB of HBM per device.

```python
import jax
import jax.numpy as jnp
from jax import lax

FF = 20480
RANK = 16
ROWS = 32
WORLD = 512


def place_ends(array, stream_key, smallest, high):
    extent = array.shape
    spot = [jax.random.randint(jax.random.fold_in(stream_key, axis), (), 0, extent[axis]) for axis in range(len(extent))]
    array = array.at[tuple(spot)].set(smallest)
    longest = extent.index(max(extent))
    spot[longest] = (spot[longest] + 1) % extent[longest]
    return array.at[tuple(spot)].set(high)


def strengthened(drawn, key, source, target, shards_of, factor):
    def block_of(position):
        return (jnp.arange(drawn.shape[position]) // (drawn.shape[position] // shards_of)).reshape((-1,) + (1,) * (drawn.ndim - 1 - position))

    first = jax.random.permutation(key, shards_of)[block_of(target)]
    second = (block_of(target) + shards_of // 2) % shards_of
    return jnp.where((block_of(source) == first) | (block_of(source) == second), factor * drawn, drawn)


def block_scale(own_key, shape, shards, least, largest):
    loudness = 1.0
    for dim, blocks in shards:
        steps = jax.random.uniform(jax.random.fold_in(jax.random.fold_in(own_key, 6), dim), (blocks,), jnp.float32, least / len(shards), largest / len(shards))
        loudness = loudness * jnp.repeat(jnp.exp(steps), shape[dim] // blocks).reshape((-1,) + (1,) * (len(shape) - 1 - dim))
    return loudness


def scatter_about(rng, dims, scale, most, split=(), dtype=jnp.bfloat16):
    result = scale * jax.random.normal(rng, dims, jnp.float32)
    if split:
        result = result * block_scale(rng, dims, split, -0.22, 0.18)
    return jnp.clip(result, -most, most).astype(dtype)


def gaussian_with(rng, shape, deviation, most, cuts, heavy, dtype=jnp.bfloat16):
    array = deviation * jax.random.normal(rng, shape, jnp.float32)
    if cuts:
        array = array * block_scale(rng, shape, cuts, -0.22, 0.18)
    return jnp.clip(strengthened(array, jax.random.fold_in(rng, 3), *heavy), -most, most).astype(dtype)


def setup_inputs(seed: int = 0) -> dict:
    seeds = jax.random.split(jax.random.key(seed), 6)
    return {
        "gradient": gaussian_with(seeds[0], (WORLD, ROWS, FF), 1.0, 24.0, ((0, 512),), (0, 2, 512, 6.0)),
        "residual": scatter_about(seeds[1], (WORLD, ROWS, FF), 0.5, 4.0, ((0, 512),)),
        "q_prev": scatter_about(seeds[2], (FF, RANK), 1.0, 6.0, ((0, 512),), jnp.float32),
        "p_bits": place_ends(jax.random.randint(seeds[3], (WORLD, ROWS, RANK), 0, 2097152), jax.random.fold_in(seeds[3], 1), 0, 2097151).astype(jnp.int32),
        "q_bits": place_ends(jax.random.randint(seeds[4], (WORLD, FF, RANK // 2), 0, 8192), jax.random.fold_in(seeds[4], 1), 0, 8191).astype(jnp.int32),
    }


dither_width = 2.0 ** (-2)

def orthonormal(matrix):
    columns = []
    for index in range(matrix.shape[1]):
        vector = matrix[:, index]
        for earlier in columns:
            vector = vector - jnp.sum(earlier * vector) * earlier
        columns.append(vector * lax.rsqrt(jnp.sum(vector * vector)))
    return jnp.stack(columns, axis=1)

def dithered(local, noise):
    sent = (local + noise * dither_width * jnp.abs(local)).astype(jnp.bfloat16)
    sent = lax.optimization_barrier(sent)
    return sent.astype(jnp.float32)

def reference(gradient, residual, q_prev, p_bits, q_bits):

    def p_term(total, items):
        grad_rows, res_rows, bits = items
        merged = grad_rows.astype(jnp.float32) + res_rows.astype(jnp.float32)
        local = jnp.dot(merged, q_prev, precision=lax.Precision.HIGHEST, preferred_element_type=jnp.float32)
        noise = bits.astype(jnp.float32) * 2.0 ** (-21) - 0.5
        return (total + dithered(local, noise), None)
    total_p, _ = lax.scan(p_term, jnp.zeros((ROWS, RANK), jnp.float32), (gradient, residual, p_bits))
    basis = orthonormal(total_p)

    def q_term(total, items):
        grad_rows, res_rows, bits = items
        merged = grad_rows.astype(jnp.float32) + res_rows.astype(jnp.float32)
        local = lax.dot_general(merged, basis, (((0,), (0,)), ((), ())), precision=lax.Precision.HIGHEST, preferred_element_type=jnp.float32)
        low = (bits % 128).astype(jnp.float32) / 128.0
        high = (bits // 128).astype(jnp.float32) / 64.0
        noise = jnp.concatenate([low, high], axis=1) - 0.5
        return (total + dithered(local, noise), None)
    total_q, _ = lax.scan(q_term, jnp.zeros((FF, RANK), jnp.float32), (gradient, residual, q_bits))
    mean_q = total_q / WORLD

    def update(items):
        grad_rows, res_rows = items
        merged = grad_rows.astype(jnp.float32) + res_rows.astype(jnp.float32)
        approx = lax.dot_general(basis, mean_q, (((1,), (1,)), ((), ())), precision=lax.Precision.HIGHEST, preferred_element_type=jnp.float32)
        return (merged - approx).astype(jnp.bfloat16)
    new_residual = lax.map(update, (gradient, residual))
    q_next = total_q * WORLD ** (-0.5)
    return (q_next, new_residual)
```

```python
import functools

import jax
import jax.numpy as jnp
from jax import lax
from jax.experimental import pallas as pl
from jax.experimental.pallas import tpu as pltpu
from jax.sharding import Mesh, PartitionSpec as P

FF = 20480
RANK = 16
ROWS = 32
WORLD = 512
HALF = FF // 2
BLOCK = 640
STEP = 2560
WIDTH = 0.25
F32 = jnp.float32
BF16 = jnp.bfloat16
VMEM_LIMIT = 48 * 1024 * 1024


def call(body, out_shape, **kw):
    return pl.pallas_call(
        body,
        out_shape=out_shape,
        compiler_params=pltpu.CompilerParams(vmem_limit_bytes=VMEM_LIMIT),
        **kw,
    )


def parts(x, n):
    out = []
    for _ in range(n):
        p = x.astype(BF16)
        out.append(p)
        x = x - p.astype(F32)
    return out


def spread_factor(x_ref, o_ref):
    halves = []
    for g in range(2):
        t = x_ref[g * 8 : g * 8 + 8].reshape(64, 128).T
        halves.append(jnp.concatenate([t[0:40], t[40:80]], axis=1))
    packed = jnp.concatenate(halves, axis=0)
    for s in range(o_ref.shape[0]):
        o_ref[s] = packed


def left_factor(c_ref, grad_ref, res_ref, own_ref, other_ref, bits_ref, o_ref):
    c = c_ref[0]
    lane = lax.broadcasted_iota(jnp.int32, (ROWS, 128), 1)
    owner = (lane % 64) // 8
    total = jnp.zeros((ROWS, 128), F32)
    for g in range(2):
        chunks = []
        for s in range(16):
            a = own_ref[s, g * 40 : g * 40 + 40, :]
            b = other_ref[s, g * 40 : g * 40 + 40, :]
            chunks.append(jnp.where(c == 0, a, b))
            chunks.append(jnp.where(c == 0, b, a))
        factor = jnp.concatenate(chunks, axis=0)
        factor = jnp.concatenate(parts(factor, 2), axis=1)
        rows = []
        for ref in (grad_ref, res_ref):
            for e in range(8):
                z = g * 8 + e
                rows.append(ref[:, z * 1280 : z * 1280 + 1280])
        wide = jnp.concatenate(rows, axis=0)
        prod = jnp.dot(wide, factor, preferred_element_type=F32)
        prod = prod[0:256] + prod[256:512]
        prod = prod[:, 0:128] + prod[:, 128:256]
        for e in range(8):
            total = total + jnp.where(owner == e, prod[e * 32 : e * 32 + 32], 0.0)
    rank = lax.broadcasted_iota(jnp.int32, (RANK, 128), 0)
    lane = lax.broadcasted_iota(jnp.int32, (RANK, 128), 1)
    fold = jnp.where((lane // 64) * 8 + lane % 8 == rank, 1.0, 0.0).astype(F32)
    local = lax.dot_general(
        fold, total, (((1,), (1,)), ((), ())), precision=lax.Precision.HIGHEST, preferred_element_type=F32
    )
    noise = bits_ref[...].astype(F32) * 2.0 ** (-21) - 0.5
    sent = (local + noise * WIDTH * jnp.abs(local)).astype(BF16).astype(F32)
    tile = jnp.concatenate([sent[0:8], sent[8:16], jnp.zeros((8, 64), F32)], axis=1)
    for s in range(o_ref.shape[0]):
        o_ref[s] = tile


def add_and_repeat(x_ref, o_ref):
    total = x_ref[0]
    for s in range(1, x_ref.shape[0]):
        total = total + x_ref[s]
    for s in range(o_ref.shape[0]):
        o_ref[s] = total


def orthonormal(rows):
    index = lax.broadcasted_iota(jnp.int32, (RANK, 1), 0)
    for j in range(RANK):
        vector = rows[j : j + 1]
        inner = jnp.sum(rows * vector, axis=1, keepdims=True)
        square = inner[j : j + 1]
        unit = vector * lax.rsqrt(square)
        later = jnp.where(index > j, inner / square, 0.0)
        rows = jnp.where(index == j, unit, rows - later * vector)
    return rows


def right_columns(basis, grad, res, words):
    split = jnp.concatenate(parts(basis, 3), axis=0)
    split = jnp.concatenate([split, split], axis=1)
    both = jnp.concatenate([grad, res], axis=0)
    prod = jnp.dot(split, both, preferred_element_type=F32)
    local = prod[0:16] + prod[16:32] + prod[32:48]
    low = (words & 127).astype(F32) * (1.0 / 128.0)
    high = (words >> 7).astype(F32) * (1.0 / 64.0)
    noise = jnp.concatenate([low, high], axis=0) - 0.5
    return (local + noise * WIDTH * jnp.abs(local)).astype(BF16).astype(F32)


def store_blocks(sent, o_ref):
    for t in range(STEP // BLOCK):
        o_ref[t] = sent[:, t * BLOCK : t * BLOCK + BLOCK]


def right_first(c_ref, tiles_ref, grad_ref, res_ref, words_ref, basis_ref, o_ref):
    @pl.when(pl.program_id(0) == 0)
    def _():
        total = tiles_ref[0]
        for s in range(1, tiles_ref.shape[0]):
            total = total + tiles_ref[s]
        rows = jnp.concatenate([total[:, 0:32], total[:, 32:64]], axis=0)
        basis_ref[...] = orthonormal(rows)

    sent = right_columns(basis_ref[...], grad_ref[...], res_ref[...], words_ref[...])
    store_blocks(sent, o_ref)


def right_second(c_ref, basis_ref, grad_ref, res_ref, words_ref, o_ref):
    sent = right_columns(basis_ref[...], grad_ref[...], res_ref[...], words_ref[...])
    store_blocks(sent, o_ref)


def update(where_ref, basis_ref, grad_ref, res_ref, own_ref, other_ref, q_ref, o_ref):
    c, block, offset = where_ref[0], where_ref[1], where_ref[2]
    high, low = parts(basis_ref[...].T, 2)
    left = jnp.concatenate([high, low, high], axis=1)

    def columns(total_ref, base):
        for t in range(HALF // BLOCK):
            mean = total_ref[t] * (1.0 / WORLD)
            mh, ml = parts(mean, 2)
            right = jnp.concatenate([mh, mh, ml], axis=0)
            approx = jnp.dot(left, right, preferred_element_type=F32)
            at = pl.ds(pl.multiple_of(base + t * BLOCK, 128), BLOCK)
            merged = grad_ref[:, at].astype(F32) + res_ref[:, at].astype(F32)
            o_ref[:, at] = (merged - approx).astype(BF16)

    columns(own_ref, c * HALF)
    columns(other_ref, (1 - c) * HALF)
    t = block % 16
    mine = jnp.where(block // 16 == c, own_ref[t], other_ref[t])
    mine = pltpu.roll(mine, (BLOCK - offset) % BLOCK, 1)
    q_ref[...] = mine[:, 0:40] * WORLD ** (-0.5)


def exchange(blocks, axis):
    return lax.all_to_all(blocks, axis, 0, 0, tiled=True)


def shards(gradient, residual, q_prev, p_bits, q_bits):
    z, plane, group = ("zh", "zl"), ("s", "c"), ("zl", "s")
    grad, res = gradient[0], residual[0]
    p_words, q_words = p_bits[0].T, q_bits[0].T
    c = lax.axis_index("c")
    device = lax.axis_index(("zh", "zl", "s", "c"))
    swap = [(0, 1), (1, 0)]
    whole = pl.BlockSpec(memory_space=pltpu.VMEM)
    scalars = pl.BlockSpec(memory_space=pltpu.SMEM)

    with jax.named_scope("gather_q_prev"):
        qt = q_prev.T
        piece = jnp.concatenate([qt[0:8], qt[8:16], jnp.zeros((8, 48), F32)], axis=1)
        pieces = exchange(jnp.broadcast_to(piece, (16, 8, 128)), z)
        spread = call(spread_factor, jax.ShapeDtypeStruct((16, 80, 128), F32), in_specs=[whole], out_specs=whole)(pieces)
        own = exchange(spread, "s")
        other = lax.ppermute(own, "c", swap)
    with jax.named_scope("left_factor"):
        tile = call(
            left_factor,
            jax.ShapeDtypeStruct((32, 8, 128), F32),
            in_specs=[scalars] + [whole] * 5,
            out_specs=whole,
        )(c.reshape(1), grad, res, own, other, p_words)
        tile = exchange(tile, plane)
        tile = call(add_and_repeat, jax.ShapeDtypeStruct((16, 8, 128), F32), in_specs=[whole], out_specs=whole)(tile)
        tile = exchange(tile, z)
    steps = HALF // STEP
    with jax.named_scope("right_factor"):

        def grid(fixed, side, out_specs):
            def place(i, c_ref):
                return (0, (c_ref[0] if side else 1 - c_ref[0]) * steps + i)

            return pltpu.PrefetchScalarGridSpec(
                num_scalar_prefetch=1,
                grid=(steps,),
                in_specs=[pl.BlockSpec(fixed, lambda i, c_ref: (0,) * len(fixed))]
                + [pl.BlockSpec((32, STEP), place), pl.BlockSpec((32, STEP), place), pl.BlockSpec((8, STEP), place)],
                out_specs=out_specs,
            )

        blocks = pl.BlockSpec((STEP // BLOCK, 16, BLOCK), lambda i, c_ref: (i, 0, 0))
        half = jax.ShapeDtypeStruct((16, 16, BLOCK), F32)
        basis, away = call(
            right_first,
            (jax.ShapeDtypeStruct((16, 32), F32), half),
            grid_spec=grid((16, 8, 128), False, (pl.BlockSpec((16, 32), lambda i, c_ref: (0, 0)), blocks)),
        )(c.reshape(1), tile, grad, res, q_words)
        away = lax.ppermute(away, "c", swap)
        kept = call(right_second, half, grid_spec=grid((16, 32), True, blocks))(c.reshape(1), basis, grad, res, q_words)
        summed = (kept + away).reshape(32, 8, BLOCK)
        summed = exchange(summed, group)
        summed = call(add_and_repeat, jax.ShapeDtypeStruct((8, 8, BLOCK), F32), in_specs=[whole], out_specs=whole)(summed)
        summed = exchange(summed, "zh")
        summed = call(add_and_repeat, jax.ShapeDtypeStruct((32, 8, BLOCK), F32), in_specs=[whole], out_specs=whole)(summed)
        total = exchange(summed, group).reshape(16, 16, BLOCK)
        rest = lax.ppermute(total, "c", swap)
    with jax.named_scope("update"):
        where = jnp.stack([c, device // 16, (device % 16) * 40])
        q_next, updated = call(
            update,
            (jax.ShapeDtypeStruct((16, 40), F32), jax.ShapeDtypeStruct((ROWS, FF), BF16)),
            in_specs=[scalars] + [whole] * 5,
            out_specs=(whole, whole),
        )(where, basis, grad, res, total, rest)
    return (q_next.T, updated[None])


def solution(mesh):
    every = ("zh", "zl", "s", "c")
    split = Mesh(mesh.devices.reshape(8, 2, 16, 2), every)
    row, block = P(every, None), P(every, None, None)
    return jax.shard_map(
        shards,
        mesh=split,
        in_specs=(block, block, row, block, block),
        out_specs=(row, block),
        check_vma=False,
    )
```

```python
import functools

import jax
import jax.numpy as jnp
from jax import lax
from jax.experimental import pallas as pl
from jax.experimental.pallas import tpu as pltpu
from jax.sharding import Mesh, PartitionSpec as P

FF = 20480
RANK = 16
ROWS = 32
WORLD = 512
HALF = FF // 2
BLOCK = 640
STEP = 2560
WIDTH = 0.25
F32 = jnp.float32
BF16 = jnp.bfloat16
VMEM_LIMIT = 16 * 1024 * 1024


def call(body, out_shape, **kw):
    return pl.pallas_call(
        body,
        out_shape=out_shape,
        compiler_params=pltpu.CompilerParams(vmem_limit_bytes=VMEM_LIMIT),
        **kw,
    )


def parts(x, n):
    out = []
    for _ in range(n):
        p = x.astype(BF16)
        out.append(p)
        x = x - p.astype(F32)
    return out


def spread_factor(x_ref, o_ref):
    halves = []
    for g in range(2):
        t = x_ref[g * 8 : g * 8 + 8].reshape(64, 128).T
        halves.append(jnp.concatenate([t[0:40], t[40:80]], axis=1))
    packed = jnp.concatenate(halves, axis=0)
    for s in range(o_ref.shape[0]):
        o_ref[s] = packed


def left_factor(c_ref, grad_ref, res_ref, own_ref, other_ref, bits_ref, o_ref):
    c = c_ref[0]
    lane = lax.broadcasted_iota(jnp.int32, (ROWS, 128), 1)
    owner = (lane % 64) // 8
    total = jnp.zeros((ROWS, 128), F32)
    for g in range(2):
        chunks = []
        for s in range(16):
            a = own_ref[s, g * 40 : g * 40 + 40, :]
            b = other_ref[s, g * 40 : g * 40 + 40, :]
            chunks.append(jnp.where(c == 0, a, b))
            chunks.append(jnp.where(c == 0, b, a))
        factor = jnp.concatenate(chunks, axis=0)
        factor = jnp.concatenate(parts(factor, 2), axis=1)
        rows = []
        for ref in (grad_ref, res_ref):
            for e in range(8):
                z = g * 8 + e
                rows.append(ref[:, z * 1280 : z * 1280 + 1280])
        wide = jnp.concatenate(rows, axis=0)
        prod = jnp.dot(wide, factor, preferred_element_type=F32)
        prod = prod[0:256] + prod[256:512]
        prod = prod[:, 0:128] + prod[:, 128:256]
        for e in range(8):
            total = total + jnp.where(owner == e, prod[e * 32 : e * 32 + 32], 0.0)
    rank = lax.broadcasted_iota(jnp.int32, (RANK, 128), 0)
    lane = lax.broadcasted_iota(jnp.int32, (RANK, 128), 1)
    fold = jnp.where((lane // 64) * 8 + lane % 8 == rank, 1.0, 0.0).astype(F32)
    local = lax.dot_general(
        fold, total, (((1,), (1,)), ((), ())), precision=lax.Precision.HIGHEST, preferred_element_type=F32
    )
    noise = bits_ref[...].astype(F32) * 2.0 ** (-21) - 0.5
    sent = (local + noise * WIDTH * jnp.abs(local)).astype(BF16).astype(F32)
    tile = jnp.concatenate([sent[0:8], sent[8:16], jnp.zeros((8, 64), F32)], axis=1)
    for s in range(o_ref.shape[0]):
        o_ref[s] = tile


def add_and_repeat(x_ref, o_ref):
    total = x_ref[0]
    for s in range(1, x_ref.shape[0]):
        total = total + x_ref[s]
    for s in range(o_ref.shape[0]):
        o_ref[s] = total


def orthonormal(rows):
    index = lax.broadcasted_iota(jnp.int32, (RANK, 1), 0)
    for j in range(RANK):
        vector = rows[j : j + 1]
        inner = jnp.sum(rows * vector, axis=1, keepdims=True)
        square = inner[j : j + 1]
        unit = vector * lax.rsqrt(square)
        later = jnp.where(index > j, inner / square, 0.0)
        rows = jnp.where(index == j, unit, rows - later * vector)
    return rows


def right_columns(basis, grad, res, words):
    split = jnp.concatenate(parts(basis, 3), axis=0)
    split = jnp.concatenate([split, split], axis=1)
    both = jnp.concatenate([grad, res], axis=0)
    prod = jnp.dot(split, both, preferred_element_type=F32)
    local = prod[0:16] + prod[16:32] + prod[32:48]
    low = (words & 127).astype(F32) * (1.0 / 128.0)
    high = (words >> 7).astype(F32) * (1.0 / 64.0)
    noise = jnp.concatenate([low, high], axis=0) - 0.5
    return (local + noise * WIDTH * jnp.abs(local)).astype(BF16).astype(F32)


def store_blocks(sent, o_ref):
    for t in range(STEP // BLOCK):
        o_ref[t] = sent[:, t * BLOCK : t * BLOCK + BLOCK]


def right_first(c_ref, tiles_ref, grad_ref, res_ref, words_ref, basis_ref, o_ref):
    @pl.when(pl.program_id(0) == 0)
    def _():
        total = tiles_ref[0]
        for s in range(1, tiles_ref.shape[0]):
            total = total + tiles_ref[s]
        rows = jnp.concatenate([total[:, 0:32], total[:, 32:64]], axis=0)
        basis_ref[...] = orthonormal(rows)

    sent = right_columns(basis_ref[...], grad_ref[...], res_ref[...], words_ref[...])
    store_blocks(sent, o_ref)


def right_second(c_ref, basis_ref, grad_ref, res_ref, words_ref, turned_ref, o_ref):
    @pl.when(pl.program_id(0) == 0)
    def _():
        turned_ref[...] = basis_ref[...].T

    sent = right_columns(basis_ref[...], grad_ref[...], res_ref[...], words_ref[...])
    store_blocks(sent, o_ref)


def new_columns(turned_ref, grad_ref, res_ref, total_ref, o_ref):
    high, low = parts(turned_ref[...], 2)
    left = jnp.concatenate([high, low, high], axis=1)
    mean = jnp.concatenate([total_ref[t] for t in range(STEP // BLOCK)], axis=1) * (1.0 / WORLD)
    mh, ml = parts(mean, 2)
    right = jnp.concatenate([mh, mh, ml], axis=0)
    approx = jnp.dot(left, right, preferred_element_type=F32)
    merged = grad_ref[...].astype(F32) + res_ref[...].astype(F32)
    o_ref[...] = (merged - approx).astype(BF16)


def update_first(where_ref, turned_ref, grad_ref, res_ref, total_ref, o_ref):
    new_columns(turned_ref, grad_ref, res_ref, total_ref, o_ref)


def update_second(where_ref, turned_ref, grad_ref, res_ref, total_ref, own_ref, rest_ref, done_ref, q_ref, o_ref):
    @pl.when(pl.program_id(0) == 0)
    def _():
        c, block, offset = where_ref[0], where_ref[1], where_ref[2]
        mine = jnp.where(block // 16 == c, own_ref[0], rest_ref[0])
        mine = pltpu.roll(mine, (BLOCK - offset) % BLOCK, 1)
        q_ref[...] = mine[:, 0:40] * WORLD ** (-0.5)

    new_columns(turned_ref, grad_ref, res_ref, total_ref, o_ref)


def exchange(blocks, axis):
    return lax.all_to_all(blocks, axis, 0, 0, tiled=True)


def shards(gradient, residual, q_prev, p_bits, q_bits):
    z, plane, group = ("zh", "zl"), ("s", "c"), ("zl", "s")
    grad, res = gradient[0], residual[0]
    p_words, q_words = p_bits[0].T, q_bits[0].T
    c = lax.axis_index("c")
    device = lax.axis_index(("zh", "zl", "s", "c"))
    swap = [(0, 1), (1, 0)]
    whole = pl.BlockSpec(memory_space=pltpu.VMEM)
    scalars = pl.BlockSpec(memory_space=pltpu.SMEM)

    with jax.named_scope("gather_q_prev"):
        qt = q_prev.T
        piece = jnp.concatenate([qt[0:8], qt[8:16], jnp.zeros((8, 48), F32)], axis=1)
        pieces = exchange(jnp.broadcast_to(piece, (16, 8, 128)), z)
        spread = call(spread_factor, jax.ShapeDtypeStruct((16, 80, 128), F32), in_specs=[whole], out_specs=whole)(pieces)
        own = exchange(spread, "s")
        other = lax.ppermute(own, "c", swap)
    with jax.named_scope("left_factor"):
        tile = call(
            left_factor,
            jax.ShapeDtypeStruct((32, 8, 128), F32),
            in_specs=[scalars] + [whole] * 5,
            out_specs=whole,
        )(c.reshape(1), grad, res, own, other, p_words)
        tile = exchange(tile, plane)
        tile = call(add_and_repeat, jax.ShapeDtypeStruct((16, 8, 128), F32), in_specs=[whole], out_specs=whole)(tile)
        tile = exchange(tile, z)
    steps = HALF // STEP
    with jax.named_scope("right_factor"):

        def grid(fixed, side, out_specs):
            def place(i, c_ref):
                return (0, (c_ref[0] if side else 1 - c_ref[0]) * steps + i)

            return pltpu.PrefetchScalarGridSpec(
                num_scalar_prefetch=1,
                grid=(steps,),
                in_specs=[pl.BlockSpec(fixed, lambda i, c_ref: (0,) * len(fixed))]
                + [pl.BlockSpec((32, STEP), place), pl.BlockSpec((32, STEP), place), pl.BlockSpec((8, STEP), place)],
                out_specs=out_specs,
            )

        blocks = pl.BlockSpec((STEP // BLOCK, 16, BLOCK), lambda i, c_ref: (i, 0, 0))
        half = jax.ShapeDtypeStruct((16, 16, BLOCK), F32)
        basis, away = call(
            right_first,
            (jax.ShapeDtypeStruct((16, 32), F32), half),
            grid_spec=grid((16, 8, 128), False, (pl.BlockSpec((16, 32), lambda i, c_ref: (0, 0)), blocks)),
        )(c.reshape(1), tile, grad, res, q_words)
        away = lax.ppermute(away, "c", swap)
        turned, kept = call(
            right_second,
            (jax.ShapeDtypeStruct((32, 16), F32), half),
            grid_spec=grid((16, 32), True, (pl.BlockSpec((32, 16), lambda i, c_ref: (0, 0)), blocks)),
        )(c.reshape(1), basis, grad, res, q_words)
        summed = (kept + away).reshape(32, 8, BLOCK)
        summed = exchange(summed, group)
        summed = call(add_and_repeat, jax.ShapeDtypeStruct((8, 8, BLOCK), F32), in_specs=[whole], out_specs=whole)(summed)
        summed = exchange(summed, "zh")
        summed = call(add_and_repeat, jax.ShapeDtypeStruct((32, 8, BLOCK), F32), in_specs=[whole], out_specs=whole)(summed)
        total = exchange(summed, group).reshape(16, 16, BLOCK)
        rest = lax.ppermute(total, "c", swap)
    with jax.named_scope("update"):
        where = jnp.stack([c, device // 16, (device % 16) * 40])

        def columns(side):
            def place(i, w_ref):
                return (0, (w_ref[0] if side else 1 - w_ref[0]) * steps + i)

            return pl.BlockSpec((32, STEP), place)

        fixed = pl.BlockSpec((32, 16), lambda i, w_ref: (0, 0))
        blocks = pl.BlockSpec((STEP // BLOCK, 16, BLOCK), lambda i, w_ref: (i, 0, 0))
        mine = pl.BlockSpec((1, 16, BLOCK), lambda i, w_ref: (w_ref[1] % 16, 0, 0))
        done = jax.ShapeDtypeStruct((ROWS, FF), BF16)
        updated = call(
            update_first,
            done,
            grid_spec=pltpu.PrefetchScalarGridSpec(
                num_scalar_prefetch=1,
                grid=(steps,),
                in_specs=[fixed, columns(True), columns(True), blocks],
                out_specs=columns(True),
            ),
        )(where, turned, grad, res, total)
        q_next, updated = call(
            update_second,
            (jax.ShapeDtypeStruct((16, 40), F32), done),
            grid_spec=pltpu.PrefetchScalarGridSpec(
                num_scalar_prefetch=1,
                grid=(steps,),
                in_specs=[fixed, columns(False), columns(False), blocks, mine, mine, pl.BlockSpec(memory_space=pl.ANY)],
                out_specs=(pl.BlockSpec((16, 40), lambda i, w_ref: (0, 0)), columns(False)),
            ),
            input_output_aliases={7: 1},
        )(where, turned, grad, res, rest, total, rest, updated)
    return (q_next.T, updated[None])


def solution(mesh):
    every = ("zh", "zl", "s", "c")
    split = Mesh(mesh.devices.reshape(8, 2, 16, 2), every)
    row, block = P(every, None), P(every, None, None)
    return jax.shard_map(
        shards,
        mesh=split,
        in_specs=(block, block, row, block, block),
        out_specs=(row, block),
        check_vma=False,
    )
```

```python
import functools

import jax
import jax.numpy as jnp
from jax import lax
from jax.experimental import pallas as pl
from jax.experimental.pallas import tpu as pltpu
from jax.sharding import Mesh, PartitionSpec as P

FF = 20480
RANK = 16
ROWS = 32
WORLD = 512
HALF = FF // 2
BLOCK = 640
STEP = 2560
WIDTH = 0.25
F32 = jnp.float32
BF16 = jnp.bfloat16
VMEM_LIMIT = 16 * 1024 * 1024


def call(body, out_shape, **kw):
    return pl.pallas_call(
        body,
        out_shape=out_shape,
        compiler_params=pltpu.CompilerParams(vmem_limit_bytes=VMEM_LIMIT),
        **kw,
    )


def parts(x, n):
    out = []
    for _ in range(n):
        p = x.astype(BF16)
        out.append(p)
        x = x - p.astype(F32)
    return out


def pack_factor(q_ref, o_ref):
    flat = jnp.concatenate([q_ref[r : r + 1, :] for r in range(RANK)], axis=1)
    for z in range(o_ref.shape[0]):
        o_ref[z] = flat


def spread_factor(x_ref, o_ref):
    pieces = x_ref[:, 0, :]
    halves = []
    for g in range(2):
        rows = [pieces[g * 8 : g * 8 + 8, r * 40 : r * 40 + 40] for r in range(RANK)]
        halves.append(jnp.concatenate(rows, axis=0).T)
    packed = jnp.concatenate(halves, axis=0)
    for s in range(o_ref.shape[0]):
        o_ref[s] = packed


def left_factor(c_ref, grad_ref, res_ref, own_ref, other_ref, bits_ref, o_ref):
    c = c_ref[0]
    lane = lax.broadcasted_iota(jnp.int32, (ROWS, 128), 1)
    owner = lane % 8
    total = jnp.zeros((ROWS, 128), F32)
    for g in range(2):
        chunks = []
        for s in range(16):
            a = own_ref[s, g * 40 : g * 40 + 40, :]
            b = other_ref[s, g * 40 : g * 40 + 40, :]
            chunks.append(jnp.where(c == 0, a, b))
            chunks.append(jnp.where(c == 0, b, a))
        factor = jnp.concatenate(chunks, axis=0)
        factor = jnp.concatenate(parts(factor, 2), axis=1)
        rows = [ref[:, z * 1280 : z * 1280 + 1280] for ref in (grad_ref, res_ref) for z in range(g * 8, g * 8 + 8)]
        prod = jnp.dot(jnp.concatenate(rows, axis=0), factor, preferred_element_type=F32)
        prod = prod[0:256] + prod[256:512]
        prod = prod[:, 0:128] + prod[:, 128:256]
        for e in range(8):
            total = total + jnp.where(owner == e, prod[e * 32 : e * 32 + 32], 0.0)
    rank = lax.broadcasted_iota(jnp.int32, (RANK, 128), 0)
    lane = lax.broadcasted_iota(jnp.int32, (RANK, 128), 1)
    fold = jnp.where(lane // 8 == rank, 1.0, 0.0).astype(F32)
    local = lax.dot_general(
        fold, total, (((1,), (1,)), ((), ())), precision=lax.Precision.HIGHEST, preferred_element_type=F32
    )
    noise = bits_ref[...].astype(F32) * 2.0 ** (-21) - 0.5
    sent = (local + noise * WIDTH * jnp.abs(local)).astype(BF16).astype(F32)
    tile = jnp.concatenate([sent[r : r + 4] for r in range(0, RANK, 4)], axis=1)
    for s in range(o_ref.shape[0]):
        o_ref[s] = tile


def add_and_repeat(x_ref, o_ref):
    total = x_ref[0]
    for s in range(1, x_ref.shape[0]):
        total = total + x_ref[s]
    for s in range(o_ref.shape[0]):
        o_ref[s] = total


def orthonormal(rows):
    index = lax.broadcasted_iota(jnp.int32, (RANK, 1), 0)
    for j in range(RANK):
        vector = rows[j : j + 1]
        inner = jnp.sum(rows * vector, axis=1, keepdims=True)
        square = inner[j : j + 1]
        unit = vector * lax.rsqrt(square)
        later = jnp.where(index > j, inner / square, 0.0)
        rows = jnp.where(index == j, unit, rows - later * vector)
    return rows


def right_columns(basis, grad, res, words):
    split = jnp.concatenate(parts(basis, 3), axis=0)
    split = jnp.concatenate([split, split], axis=1)
    both = jnp.concatenate([grad, res], axis=0)
    prod = jnp.dot(split, both, preferred_element_type=F32)
    local = prod[0:16] + prod[16:32] + prod[32:48]
    low = (words & 127).astype(F32) * (1.0 / 128.0)
    high = (words >> 7).astype(F32) * (1.0 / 64.0)
    noise = jnp.concatenate([low, high], axis=0) - 0.5
    return (local + noise * WIDTH * jnp.abs(local)).astype(BF16).astype(F32)


def half_columns(side, basis, grad_ref, res_ref, words_ref, o_ref):
    for i in range(HALF // STEP):
        at = pl.ds(pl.multiple_of(side * HALF + i * STEP, STEP), STEP)
        sent = right_columns(basis, grad_ref[:, at], res_ref[:, at], words_ref[:, at])
        for t in range(STEP // BLOCK):
            o_ref[i * (STEP // BLOCK) + t] = sent[:, t * BLOCK : t * BLOCK + BLOCK]


def right_first(c_ref, tiles_ref, grad_ref, res_ref, words_ref, basis_ref, o_ref):
    total = tiles_ref[0]
    for s in range(1, tiles_ref.shape[0]):
        total = total + tiles_ref[s]
    rows = jnp.concatenate([total[:, r : r + 32] for r in range(0, 128, 32)], axis=0)
    basis = orthonormal(rows)
    basis_ref[...] = basis
    half_columns(1 - c_ref[0], basis, grad_ref, res_ref, words_ref, o_ref)


def right_second(c_ref, basis_ref, grad_ref, res_ref, words_ref, turned_ref, o_ref):
    turned_ref[...] = basis_ref[...].T
    half_columns(c_ref[0], basis_ref[...], grad_ref, res_ref, words_ref, o_ref)


def new_columns(side, turned_ref, grad_ref, res_ref, total_ref, o_ref, made_ref, sems):
    high, low = parts(turned_ref[...] * (1.0 / WORLD), 2)
    left = jnp.concatenate([high, low, high], axis=1)
    copies = []
    for i in range(HALF // STEP):
        at = pl.ds(pl.multiple_of(side * HALF + i * STEP, STEP), STEP)
        here = pl.ds(i * STEP, STEP)
        blocks = [total_ref[t] for t in range(i * STEP // BLOCK, (i + 1) * STEP // BLOCK)]
        th, tl = parts(jnp.concatenate(blocks, axis=1), 2)
        right = jnp.concatenate([th, th, tl], axis=0)
        approx = jnp.dot(left, right, preferred_element_type=F32)
        merged = grad_ref[:, at].astype(F32) + res_ref[:, at].astype(F32)
        made_ref[:, here] = (merged - approx).astype(BF16)
        copy = pltpu.make_async_copy(made_ref.at[:, here], o_ref.at[:, at], sems.at[i])
        copy.start()
        copies.append(copy)
    return copies


def update_first(where_ref, turned_ref, grad_ref, res_ref, own_ref, o_ref, made_ref, sems):
    for copy in new_columns(where_ref[0], turned_ref, grad_ref, res_ref, own_ref, o_ref, made_ref, sems):
        copy.wait()


def update_second(
    where_ref, turned_ref, grad_ref, res_ref, own_ref, rest_ref, done_ref, q_ref, o_ref, made_ref, sems
):
    c, block, offset = where_ref[0], where_ref[1], where_ref[2]
    copies = new_columns(1 - c, turned_ref, grad_ref, res_ref, rest_ref, o_ref, made_ref, sems)
    t = block % 16
    mine = jnp.where(block // 16 == c, own_ref[t], rest_ref[t])
    mine = pltpu.roll(mine, (BLOCK - offset) % BLOCK, 1)
    q_ref[...] = mine[:, 0:40] * WORLD ** (-0.5)
    for copy in copies:
        copy.wait()


def exchange(blocks, axis):
    return lax.all_to_all(blocks, axis, 0, 0, tiled=True)


def shards(gradient, residual, q_prev, p_bits, q_bits):
    z, plane, group = ("zh", "zl"), ("s", "c"), ("zl", "s")
    grad, res = gradient[0], residual[0]
    p_words, q_words = p_bits[0].T, q_bits[0].T
    c = lax.axis_index("c")
    device = lax.axis_index(("zh", "zl", "s", "c"))
    swap = [(0, 1), (1, 0)]
    whole = pl.BlockSpec(memory_space=pltpu.VMEM)
    far = pl.BlockSpec(memory_space=pl.ANY)
    scalars = pl.BlockSpec(memory_space=pltpu.SMEM)

    with jax.named_scope("gather_q_prev"):
        pieces = call(pack_factor, jax.ShapeDtypeStruct((16, 1, 640), F32), in_specs=[whole], out_specs=whole)(q_prev.T)
        pieces = exchange(pieces, z)
        spread = call(
            spread_factor,
            jax.ShapeDtypeStruct((16, 80, 128), F32),
            in_specs=[whole],
            out_specs=whole,
            cost_estimate=pl.CostEstimate(flops=10**11, bytes_accessed=10**8, transcendentals=0),
        )(pieces)
        own = exchange(spread, "s")
        other = lax.ppermute(own, "c", swap)
    with jax.named_scope("left_factor"):
        tile = call(
            left_factor,
            jax.ShapeDtypeStruct((32, 4, 128), F32),
            in_specs=[scalars] + [whole] * 5,
            out_specs=whole,
        )(c.reshape(1), grad, res, own, other, p_words)
        tile = exchange(tile, plane)
        tile = call(add_and_repeat, jax.ShapeDtypeStruct((16, 4, 128), F32), in_specs=[whole], out_specs=whole)(tile)
        tile = exchange(tile, z)
    steps = HALF // STEP
    with jax.named_scope("right_factor"):
        half = jax.ShapeDtypeStruct((16, 16, BLOCK), F32)
        basis, away = call(
            right_first,
            (jax.ShapeDtypeStruct((16, 32), F32), half),
            in_specs=[scalars] + [whole] * 4,
            out_specs=(whole, whole),
        )(c.reshape(1), tile, grad, res, q_words)
        away = lax.ppermute(away, "c", swap)
        turned, kept = call(
            right_second,
            (jax.ShapeDtypeStruct((32, 16), F32), half),
            in_specs=[scalars] + [whole] * 4,
            out_specs=(whole, whole),
        )(c.reshape(1), basis, grad, res, q_words)
        summed = (kept + away).reshape(32, 8, BLOCK)
        summed = exchange(summed, group)
        summed = call(add_and_repeat, jax.ShapeDtypeStruct((8, 8, BLOCK), F32), in_specs=[whole], out_specs=whole)(summed)
        summed = exchange(summed, "zh")
        summed = call(add_and_repeat, jax.ShapeDtypeStruct((32, 8, BLOCK), F32), in_specs=[whole], out_specs=whole)(summed)
        total = exchange(summed, group).reshape(16, 16, BLOCK)
        rest = lax.ppermute(total, "c", swap)
    with jax.named_scope("update"):
        where = jnp.stack([c, device // 16, (device % 16) * 40])
        done = jax.ShapeDtypeStruct((ROWS, FF), BF16)
        room = [pltpu.VMEM((ROWS, HALF), BF16), pltpu.SemaphoreType.DMA((steps,))]
        updated = call(
            update_first, done, in_specs=[scalars] + [whole] * 4, out_specs=far, scratch_shapes=room
        )(where, turned, grad, res, total)
        q_next, updated = call(
            update_second,
            (jax.ShapeDtypeStruct((16, 40), F32), done),
            in_specs=[scalars] + [whole] * 5 + [far],
            out_specs=(whole, far),
            scratch_shapes=room,
            input_output_aliases={6: 1},
        )(where, turned, grad, res, total, rest, updated)
    return (q_next.T, updated[None])


def solution(mesh):
    every = ("zh", "zl", "s", "c")
    split = Mesh(mesh.devices.reshape(8, 2, 16, 2), every)
    row, block = P(every, None), P(every, None, None)
    return jax.shard_map(
        shards,
        mesh=split,
        in_specs=(block, block, row, block, block),
        out_specs=(row, block),
        check_vma=False,
    )
```

```python
import functools

import jax
import jax.numpy as jnp
from jax import lax
from jax.experimental import pallas as pl
from jax.experimental.pallas import tpu as pltpu
from jax.sharding import Mesh, PartitionSpec as P

FF = 20480
RANK = 16
ROWS = 32
WORLD = 512
HALF = FF // 2
BLOCK = 640
STEP = 2560
WIDTH = 0.25
F32 = jnp.float32
BF16 = jnp.bfloat16
VMEM_LIMIT = 16 * 1024 * 1024


def call(body, out_shape, **kw):
    return pl.pallas_call(
        body,
        out_shape=out_shape,
        compiler_params=pltpu.CompilerParams(vmem_limit_bytes=VMEM_LIMIT),
        **kw,
    )


def parts(x, n):
    out = []
    for _ in range(n):
        p = x.astype(BF16)
        out.append(p)
        x = x - p.astype(F32)
    return out


def pack_factor(q_ref, o_ref):
    flat = jnp.concatenate([q_ref[r : r + 1, :] for r in range(RANK)], axis=1)
    for z in range(o_ref.shape[0]):
        o_ref[z] = flat


def spread_factor(x_ref, o_ref):
    pieces = x_ref[:, 0, :]
    halves = []
    for g in range(2):
        rows = [pieces[g * 8 : g * 8 + 8, r * 40 : r * 40 + 40] for r in range(RANK)]
        halves.append(jnp.concatenate(rows, axis=0).T)
    packed = jnp.concatenate(halves, axis=0)
    for s in range(o_ref.shape[0]):
        o_ref[s] = packed


def left_factor(grad_ref, res_ref, own_ref, other_ref, bits_ref, o_ref):
    c = lax.axis_index("c")
    lane = lax.broadcasted_iota(jnp.int32, (ROWS, 128), 1)
    owner = lane % 8
    total = jnp.zeros((ROWS, 128), F32)
    for g in range(2):
        chunks = []
        for s in range(16):
            a = own_ref[s, g * 40 : g * 40 + 40, :]
            b = other_ref[s, g * 40 : g * 40 + 40, :]
            chunks.append(jnp.where(c == 0, a, b))
            chunks.append(jnp.where(c == 0, b, a))
        factor = jnp.concatenate(chunks, axis=0)
        factor = jnp.concatenate(parts(factor, 2), axis=1)
        rows = [ref[:, z * 1280 : z * 1280 + 1280] for ref in (grad_ref, res_ref) for z in range(g * 8, g * 8 + 8)]
        prod = jnp.dot(jnp.concatenate(rows, axis=0), factor, preferred_element_type=F32)
        prod = prod[0:256] + prod[256:512]
        prod = prod[:, 0:128] + prod[:, 128:256]
        for e in range(8):
            total = total + jnp.where(owner == e, prod[e * 32 : e * 32 + 32], 0.0)
    rank = lax.broadcasted_iota(jnp.int32, (RANK, 128), 0)
    lane = lax.broadcasted_iota(jnp.int32, (RANK, 128), 1)
    fold = jnp.where(lane // 8 == rank, 1.0, 0.0).astype(F32)
    local = lax.dot_general(
        fold, total, (((1,), (1,)), ((), ())), precision=lax.Precision.HIGHEST, preferred_element_type=F32
    )
    noise = bits_ref[...].astype(F32) * 2.0 ** (-21) - 0.5
    sent = (local + noise * WIDTH * jnp.abs(local)).astype(BF16).astype(F32)
    tile = jnp.concatenate([sent[r : r + 4] for r in range(0, RANK, 4)], axis=1)
    for s in range(o_ref.shape[0]):
        o_ref[s] = tile


def add_and_repeat(x_ref, o_ref):
    total = x_ref[0]
    for s in range(1, x_ref.shape[0]):
        total = total + x_ref[s]
    for s in range(o_ref.shape[0]):
        o_ref[s] = total


def orthonormal(rows):
    index = lax.broadcasted_iota(jnp.int32, (RANK, 1), 0)
    for j in range(RANK):
        vector = rows[j : j + 1]
        inner = jnp.sum(rows * vector, axis=1, keepdims=True)
        square = inner[j : j + 1]
        unit = vector * lax.rsqrt(square)
        later = jnp.where(index > j, inner / square, 0.0)
        rows = jnp.where(index == j, unit, rows - later * vector)
    return rows


def right_columns(basis, grad, res, words):
    split = jnp.concatenate(parts(basis, 3), axis=0)
    split = jnp.concatenate([split, split], axis=1)
    both = jnp.concatenate([grad, res], axis=0)
    prod = jnp.dot(split, both, preferred_element_type=F32)
    local = prod[0:16] + prod[16:32] + prod[32:48]
    low = (words & 127).astype(F32) * (1.0 / 128.0)
    high = (words >> 7).astype(F32) * (1.0 / 64.0)
    noise = jnp.concatenate([low, high], axis=0) - 0.5
    return (local + noise * WIDTH * jnp.abs(local)).astype(BF16).astype(F32)


def half_columns(side, basis, grad_ref, res_ref, words_ref, o_ref):
    for i in range(HALF // STEP):
        at = pl.ds(pl.multiple_of(side * HALF + i * STEP, STEP), STEP)
        sent = right_columns(basis, grad_ref[:, at], res_ref[:, at], words_ref[:, at])
        for t in range(STEP // BLOCK):
            o_ref[i * (STEP // BLOCK) + t] = sent[:, t * BLOCK : t * BLOCK + BLOCK]


def right_first(tiles_ref, grad_ref, res_ref, words_ref, basis_ref, o_ref):
    total = tiles_ref[0]
    for s in range(1, tiles_ref.shape[0]):
        total = total + tiles_ref[s]
    rows = jnp.concatenate([total[:, r : r + 32] for r in range(0, 128, 32)], axis=0)
    basis = orthonormal(rows)
    basis_ref[...] = basis
    half_columns(1 - lax.axis_index("c"), basis, grad_ref, res_ref, words_ref, o_ref)


def right_second(basis_ref, grad_ref, res_ref, words_ref, turned_ref, o_ref):
    turned_ref[...] = basis_ref[...].T
    half_columns(lax.axis_index("c"), basis_ref[...], grad_ref, res_ref, words_ref, o_ref)


def new_columns(side, turned_ref, grad_ref, res_ref, total_ref, o_ref, made_ref, sems):
    high, low = parts(turned_ref[...] * (1.0 / WORLD), 2)
    left = jnp.concatenate([high, low, high], axis=1)
    copies = []
    for i in range(HALF // STEP):
        at = pl.ds(pl.multiple_of(side * HALF + i * STEP, STEP), STEP)
        here = pl.ds(i * STEP, STEP)
        blocks = [total_ref[t] for t in range(i * STEP // BLOCK, (i + 1) * STEP // BLOCK)]
        th, tl = parts(jnp.concatenate(blocks, axis=1), 2)
        right = jnp.concatenate([th, th, tl], axis=0)
        approx = jnp.dot(left, right, preferred_element_type=F32)
        merged = grad_ref[:, at].astype(F32) + res_ref[:, at].astype(F32)
        made_ref[:, here] = (merged - approx).astype(BF16)
        copy = pltpu.make_async_copy(made_ref.at[:, here], o_ref.at[:, at], sems.at[i])
        copy.start()
        copies.append(copy)
    return copies


def update_first(turned_ref, grad_ref, res_ref, own_ref, o_ref, made_ref, sems):
    for copy in new_columns(lax.axis_index("c"), turned_ref, grad_ref, res_ref, own_ref, o_ref, made_ref, sems):
        copy.wait()


def update_second(
    turned_ref, grad_ref, res_ref, own_ref, rest_ref, done_ref, q_ref, o_ref, made_ref, sems
):
    c = lax.axis_index("c")
    device = ((lax.axis_index("zh") * 2 + lax.axis_index("zl")) * 16 + lax.axis_index("s")) * 2 + c
    block, offset = device // 16, (device % 16) * 40
    copies = new_columns(1 - c, turned_ref, grad_ref, res_ref, rest_ref, o_ref, made_ref, sems)
    t = block % 16
    mine = jnp.where(block // 16 == c, own_ref[t], rest_ref[t])
    mine = pltpu.roll(mine, (BLOCK - offset) % BLOCK, 1)
    q_ref[...] = mine[:, 0:40] * WORLD ** (-0.5)
    for copy in copies:
        copy.wait()


def exchange(blocks, axis):
    return lax.all_to_all(blocks, axis, 0, 0, tiled=True)


def shards(gradient, residual, q_prev, p_bits, q_bits):
    z, plane, group = ("zh", "zl"), ("s", "c"), ("zl", "s")
    grad, res = gradient[0], residual[0]
    p_words, q_words = p_bits[0].T, q_bits[0].T
    swap = [(0, 1), (1, 0)]
    whole = pl.BlockSpec(memory_space=pltpu.VMEM)
    far = pl.BlockSpec(memory_space=pl.ANY)

    with jax.named_scope("gather_q_prev"):
        pieces = call(pack_factor, jax.ShapeDtypeStruct((16, 1, 640), F32), in_specs=[whole], out_specs=whole)(q_prev.T)
        pieces = exchange(pieces, z)
        spread = call(
            spread_factor,
            jax.ShapeDtypeStruct((16, 80, 128), F32),
            in_specs=[whole],
            out_specs=whole,
            cost_estimate=pl.CostEstimate(flops=10**11, bytes_accessed=10**8, transcendentals=0),
        )(pieces)
        own = exchange(spread, "s")
        other = lax.ppermute(own, "c", swap)
    with jax.named_scope("left_factor"):
        tile = call(
            left_factor,
            jax.ShapeDtypeStruct((32, 4, 128), F32),
            in_specs=[whole] * 5,
            out_specs=whole,
        )(grad, res, own, other, p_words)
        tile = exchange(tile, plane)
        tile = call(add_and_repeat, jax.ShapeDtypeStruct((16, 4, 128), F32), in_specs=[whole], out_specs=whole)(tile)
        tile = exchange(tile, z)
    steps = HALF // STEP
    with jax.named_scope("right_factor"):
        half = jax.ShapeDtypeStruct((16, 16, BLOCK), F32)
        basis, away = call(
            right_first,
            (jax.ShapeDtypeStruct((16, 32), F32), half),
            in_specs=[whole] * 4,
            out_specs=(whole, whole),
        )(tile, grad, res, q_words)
        away = lax.ppermute(away, "c", swap)
        turned, kept = call(
            right_second,
            (jax.ShapeDtypeStruct((32, 16), F32), half),
            in_specs=[whole] * 4,
            out_specs=(whole, whole),
        )(basis, grad, res, q_words)
        summed = (kept + away).reshape(32, 8, BLOCK)
        summed = exchange(summed, group)
        summed = call(add_and_repeat, jax.ShapeDtypeStruct((8, 8, BLOCK), F32), in_specs=[whole], out_specs=whole)(summed)
        summed = exchange(summed, "zh")
        summed = call(add_and_repeat, jax.ShapeDtypeStruct((32, 8, BLOCK), F32), in_specs=[whole], out_specs=whole)(summed)
        total = exchange(summed, group).reshape(16, 16, BLOCK)
        rest = lax.ppermute(total, "c", swap)
    with jax.named_scope("update"):
        done = jax.ShapeDtypeStruct((ROWS, FF), BF16)
        room = [pltpu.VMEM((ROWS, HALF), BF16), pltpu.SemaphoreType.DMA((steps,))]
        updated = call(
            update_first, done, in_specs=[whole] * 4, out_specs=far, scratch_shapes=room
        )(turned, grad, res, total)
        q_next, updated = call(
            update_second,
            (jax.ShapeDtypeStruct((16, 40), F32), done),
            in_specs=[whole] * 5 + [far],
            out_specs=(whole, far),
            scratch_shapes=room,
            input_output_aliases={5: 1},
        )(turned, grad, res, total, rest, updated)
    return (q_next.T, updated[None])


def solution(mesh):
    every = ("zh", "zl", "s", "c")
    split = Mesh(mesh.devices.reshape(8, 2, 16, 2), every)
    row, block = P(every, None), P(every, None, None)
    return jax.shard_map(
        shards,
        mesh=split,
        in_specs=(block, block, row, block, block),
        out_specs=(row, block),
        check_vma=False,
    )
```

```python
import functools

import jax
import jax.numpy as jnp
from jax import lax
from jax.experimental import pallas as pl
from jax.experimental.pallas import tpu as pltpu
from jax.sharding import Mesh, PartitionSpec as P

FF = 20480
RANK = 16
ROWS = 32
WORLD = 512
HALF = FF // 2
BLOCK = 640
STEP = 2560
SHARE = 2560
WIDTH = 0.25
F32 = jnp.float32
BF16 = jnp.bfloat16
VMEM_LIMIT = 16 * 1024 * 1024


def call(body, out_shape, limit=VMEM_LIMIT, **kw):
    return pl.pallas_call(
        body,
        out_shape=out_shape,
        compiler_params=pltpu.CompilerParams(vmem_limit_bytes=limit),
        **kw,
    )


def parts(x, n):
    out = []
    for _ in range(n):
        p = x.astype(BF16)
        out.append(p)
        x = x - p.astype(F32)
    return out


def pack_factor(q_ref, o_ref):
    flat = jnp.concatenate([q_ref[r : r + 1, :] for r in range(RANK)], axis=1)
    for z in range(o_ref.shape[0]):
        o_ref[z] = flat


def share(far_grad_ref, far_res_ref, far_words_ref, bits_ref, far_ref, grad_ref, res_ref, words_ref, o_ref, sems):
    pairs = ((far_grad_ref, grad_ref), (far_res_ref, res_ref), (far_words_ref, words_ref))
    copies = []
    for i in range(FF // SHARE):
        at = pl.ds(i * SHARE, SHARE)
        copies.append([pltpu.make_async_copy(far.at[:, at], near.at[:, at], sems.at[i, k]) for k, (far, near) in enumerate(pairs)])
        for copy in copies[i]:
            copy.start()
    bits = bits_ref[...].astype(F32)
    o_ref[0:8, FF:] = jnp.concatenate([bits[0:8], bits[8:16], jnp.zeros((8, 64), F32)], axis=1)
    for i in range(FF // SHARE):
        at = pl.ds(i * SHARE, SHARE)
        for copy in copies[i]:
            copy.wait()
        o_ref[0:ROWS, at] = grad_ref[:, at].astype(F32) + res_ref[:, at].astype(F32)
        o_ref[ROWS : ROWS + 8, at] = words_ref[:, at].astype(F32)
        last = FF + 128 if i == FF // SHARE - 1 else i * SHARE + SHARE
        here = pl.ds(i * SHARE, last - i * SHARE)
        copies.append(pltpu.make_async_copy(o_ref.at[:, here], far_ref.at[:, here], sems.at[i, 3]))
        copies[-1].start()
    for copy in copies[FF // SHARE :]:
        copy.wait()


def spread_factor(x_ref, o_ref):
    pieces = x_ref[:, 0, :]
    for half in range(2):
        rows = [pieces[:, r * 40 : r * 40 + 40] for r in range(half * 8, half * 8 + 8)]
        packed = jnp.concatenate(rows, axis=0).T
        for s in range(16):
            o_ref[s * 2 + half] = packed


def left_factor(grad_ref, res_ref, other_ref, factor_ref, bits_ref, o_ref):
    c = lax.axis_index("c")
    factor = jnp.concatenate(parts(factor_ref[...].reshape(1280, 128), 2), axis=1)
    owner = lax.broadcasted_iota(jnp.int32, (ROWS, 128), 1) % 16
    totals = [jnp.zeros((ROWS, 128), F32), jnp.zeros((ROWS, 128), F32)]
    for z in range(0, 16, 4):
        places = [slice(k * 1280, k * 1280 + 1280) for k in range(z, z + 4)]
        split = [parts(other_ref[0:ROWS, at], 2) for at in places]
        rows = [grad_ref[:, at] for at in places] + [res_ref[:, at] for at in places]
        rows += [high for high, _ in split] + [low for _, low in split]
        prod = jnp.dot(jnp.concatenate(rows, axis=0), factor, preferred_element_type=F32)
        prod = prod[:, 0:128] + prod[:, 128:256]
        for w in range(2):
            both = prod[w * 256 : w * 256 + 128] + prod[w * 256 + 128 : w * 256 + 256]
            for k in range(4):
                totals[w] = totals[w] + jnp.where(owner == z + k, both[k * 32 : k * 32 + 32], 0.0)
    rank = lax.broadcasted_iota(jnp.int32, (8, 128), 0)
    lane = lax.broadcasted_iota(jnp.int32, (8, 128), 1)
    fold = jnp.where(lane // 16 == rank, 1.0, 0.0).astype(F32)
    here = bits_ref[...].astype(F32)
    there = other_ref[0:8, FF:]
    bits = (
        jnp.where(c == 0, here[0:8], here[8:16]),
        jnp.where(c == 0, there[:, 0:32], there[:, 32:64]),
    )
    sent = jnp.zeros((8, 32), F32)
    for w in range(2):
        local = lax.dot_general(
            fold, totals[w], (((1,), (1,)), ((), ())), precision=lax.Precision.HIGHEST, preferred_element_type=F32
        )
        noise = bits[w] * 2.0 ** (-21) - 0.5
        sent = sent + (local + noise * WIDTH * jnp.abs(local)).astype(BF16).astype(F32)
    tile = jnp.concatenate([sent[r : r + 2] for r in range(0, 8, 2)], axis=1)
    for s in range(o_ref.shape[0]):
        o_ref[s] = tile


def add_left(x_ref, o_ref):
    halves = []
    for c in range(2):
        total = x_ref[c]
        for s in range(1, 16):
            total = total + x_ref[s * 2 + c]
        halves.append(total)
    both = jnp.concatenate(halves, axis=0)
    for z in range(o_ref.shape[0]):
        o_ref[z] = both


def add_and_repeat(x_ref, o_ref):
    total = x_ref[0]
    for s in range(1, x_ref.shape[0]):
        total = total + x_ref[s]
    for s in range(o_ref.shape[0]):
        o_ref[s] = total


def orthonormal(rows):
    index = lax.broadcasted_iota(jnp.int32, (RANK, 1), 0)
    for j in range(RANK):
        vector = rows[j : j + 1]
        inner = jnp.sum(rows * vector, axis=1, keepdims=True)
        square = inner[j : j + 1]
        unit = vector * lax.rsqrt(square)
        later = jnp.where(index > j, inner / square, 0.0)
        rows = jnp.where(index == j, unit, rows - later * vector)
    return rows


def right_columns(split, first, second, words):
    prod = jnp.dot(split, jnp.concatenate([first, second], axis=0), preferred_element_type=F32)
    local = prod[0:16] + prod[16:32] + prod[32:48]
    low = (words & 127).astype(F32) * (1.0 / 128.0)
    high = (words >> 7).astype(F32) * (1.0 / 64.0)
    noise = jnp.concatenate([low, high], axis=0) - 0.5
    return (local + noise * WIDTH * jnp.abs(local)).astype(BF16).astype(F32)


def right_factor(tiles_ref, grad_ref, res_ref, words_ref, other_ref, turned_ref, o_ref):
    total = tiles_ref[0]
    for s in range(1, tiles_ref.shape[0]):
        total = total + tiles_ref[s]
    rows = [total[c * 2 : c * 2 + 2, q * 32 : q * 32 + 32] for c in range(2) for q in range(4)]
    basis = orthonormal(jnp.concatenate(rows, axis=0))
    turned_ref[...] = basis.T
    split = jnp.concatenate(parts(basis, 3), axis=0)
    split = jnp.concatenate([split, split], axis=1)
    base = lax.axis_index("c") * HALF
    for i in range(HALF // STEP):
        at = pl.ds(pl.multiple_of(base + i * STEP, STEP), STEP)
        sent = right_columns(split, grad_ref[:, at], res_ref[:, at], words_ref[:, at])
        high, low = parts(other_ref[0:ROWS, at], 2)
        sent = sent + right_columns(split, high, low, other_ref[ROWS : ROWS + 8, at].astype(jnp.int32))
        for t in range(STEP // BLOCK):
            o_ref[i * (STEP // BLOCK) + t] = sent[:, t * BLOCK : t * BLOCK + BLOCK]


def new_columns(side, turned_ref, grad_ref, res_ref, total_ref, o_ref, made_ref, sems):
    high, low = parts(turned_ref[...] * (1.0 / WORLD), 2)
    left = jnp.concatenate([high, low, high], axis=1)
    copies = []
    for i in range(HALF // STEP):
        at = pl.ds(pl.multiple_of(side * HALF + i * STEP, STEP), STEP)
        here = pl.ds(i * STEP, STEP)
        blocks = [total_ref[t] for t in range(i * STEP // BLOCK, (i + 1) * STEP // BLOCK)]
        th, tl = parts(jnp.concatenate(blocks, axis=1), 2)
        right = jnp.concatenate([th, th, tl], axis=0)
        approx = jnp.dot(left, right, preferred_element_type=F32)
        merged = grad_ref[:, at].astype(F32) + res_ref[:, at].astype(F32)
        made_ref[:, here] = (merged - approx).astype(BF16)
        copy = pltpu.make_async_copy(made_ref.at[:, here], o_ref.at[:, at], sems.at[i])
        copy.start()
        copies.append(copy)
    return copies


def update_first(turned_ref, grad_ref, res_ref, own_ref, o_ref, made_ref, sems):
    for copy in new_columns(lax.axis_index("c"), turned_ref, grad_ref, res_ref, own_ref, o_ref, made_ref, sems):
        copy.wait()


def update_second(
    turned_ref, grad_ref, res_ref, own_ref, rest_ref, done_ref, q_ref, o_ref, made_ref, sems
):
    c = lax.axis_index("c")
    device = ((lax.axis_index("zh") * 2 + lax.axis_index("zl")) * 16 + lax.axis_index("s")) * 2 + c
    block, offset = device // 16, (device % 16) * 40
    copies = new_columns(1 - c, turned_ref, grad_ref, res_ref, rest_ref, o_ref, made_ref, sems)
    t = block % 16
    mine = jnp.where(block // 16 == c, own_ref[t], rest_ref[t])
    mine = pltpu.roll(mine, (BLOCK - offset) % BLOCK, 1)
    q_ref[...] = mine[:, 0:40] * WORLD ** (-0.5)
    for copy in copies:
        copy.wait()


def exchange(blocks, axis):
    return lax.all_to_all(blocks, axis, 0, 0, tiled=True)


def shards(gradient, residual, q_prev, p_bits, q_bits):
    z, plane, group = ("zh", "zl"), ("s", "c"), ("zl", "s")
    grad, res = gradient[0], residual[0]
    p_words, q_words = p_bits[0].T, q_bits[0].T
    swap = [(0, 1), (1, 0)]
    whole = pl.BlockSpec(memory_space=pltpu.VMEM)
    far = pl.BlockSpec(memory_space=pl.ANY)

    with jax.named_scope("share"):
        mine = call(
            share,
            jax.ShapeDtypeStruct((ROWS + 8, FF + 128), F32),
            limit=56 * 1024 * 1024,
            in_specs=[far, far, far, whole],
            out_specs=far,
            scratch_shapes=[
                pltpu.VMEM((ROWS, FF), BF16),
                pltpu.VMEM((ROWS, FF), BF16),
                pltpu.VMEM((8, FF), jnp.int32),
                pltpu.VMEM((ROWS + 8, FF + 128), F32),
                pltpu.SemaphoreType.DMA((FF // SHARE, 4)),
            ],
        )(grad, res, q_words, p_words)
        other = lax.ppermute(mine, "c", swap)
    with jax.named_scope("gather_q_prev"):
        pieces = call(pack_factor, jax.ShapeDtypeStruct((16, 1, 640), F32), in_specs=[whole], out_specs=whole)(q_prev.T)
        pieces = exchange(pieces, z)
        spread = call(
            spread_factor,
            jax.ShapeDtypeStruct((32, 40, 128), F32),
            in_specs=[whole],
            out_specs=whole,
            cost_estimate=pl.CostEstimate(flops=10**11, bytes_accessed=10**8, transcendentals=0),
        )(pieces)
        factor = exchange(spread, plane)
    with jax.named_scope("left_factor"):
        tile = call(left_factor, jax.ShapeDtypeStruct((32, 2, 128), F32), in_specs=[whole] * 5, out_specs=whole)(
            grad, res, other, factor, p_words
        )
        tile = exchange(tile, plane)
        tile = call(add_left, jax.ShapeDtypeStruct((16, 4, 128), F32), in_specs=[whole], out_specs=whole)(tile)
        tile = exchange(tile, z)
    steps = HALF // STEP
    with jax.named_scope("right_factor"):
        turned, summed = call(
            right_factor,
            (jax.ShapeDtypeStruct((32, 16), F32), jax.ShapeDtypeStruct((16, 16, BLOCK), F32)),
            in_specs=[whole] * 5,
            out_specs=(whole, whole),
        )(tile, grad, res, q_words, other)
        summed = summed.reshape(32, 8, BLOCK)
        summed = exchange(summed, group)
        summed = call(add_and_repeat, jax.ShapeDtypeStruct((8, 8, BLOCK), F32), in_specs=[whole], out_specs=whole)(summed)
        summed = exchange(summed, "zh")
        summed = call(add_and_repeat, jax.ShapeDtypeStruct((32, 8, BLOCK), F32), in_specs=[whole], out_specs=whole)(summed)
        total = exchange(summed, group).reshape(16, 16, BLOCK)
        rest = lax.ppermute(total, "c", swap)
    with jax.named_scope("update"):
        done = jax.ShapeDtypeStruct((ROWS, FF), BF16)
        room = [pltpu.VMEM((ROWS, HALF), BF16), pltpu.SemaphoreType.DMA((steps,))]
        updated = call(
            update_first, done, in_specs=[whole] * 4, out_specs=far, scratch_shapes=room
        )(turned, grad, res, total)
        q_next, updated = call(
            update_second,
            (jax.ShapeDtypeStruct((16, 40), F32), done),
            in_specs=[whole] * 5 + [far],
            out_specs=(whole, far),
            scratch_shapes=room,
            input_output_aliases={5: 1},
        )(turned, grad, res, total, rest, updated)
    return (q_next.T, updated[None])


def solution(mesh):
    every = ("zh", "zl", "s", "c")
    split = Mesh(mesh.devices.reshape(8, 2, 16, 2), every)
    row, block = P(every, None), P(every, None, None)
    return jax.shard_map(
        shards,
        mesh=split,
        in_specs=(block, block, row, block, block),
        out_specs=(row, block),
        check_vma=False,
    )
```

```python
import functools

import jax
import jax.numpy as jnp
from jax import lax
from jax.experimental import pallas as pl
from jax.experimental.pallas import tpu as pltpu
from jax.sharding import Mesh, PartitionSpec as P

FF = 20480
RANK = 16
ROWS = 32
WORLD = 512
HALF = FF // 2
BLOCK = 640
STEP = 2560
SHARE = 5120
WIDTH = 0.25
F32 = jnp.float32
BF16 = jnp.bfloat16
VMEM_LIMIT = 16 * 1024 * 1024


def call(body, out_shape, limit=VMEM_LIMIT, **kw):
    return pl.pallas_call(
        body,
        out_shape=out_shape,
        compiler_params=pltpu.CompilerParams(vmem_limit_bytes=limit),
        **kw,
    )


def parts(x, n):
    out = []
    for _ in range(n):
        p = x.astype(BF16)
        out.append(p)
        x = x - p.astype(F32)
    return out


def pack_factor(q_ref, o_ref):
    flat = jnp.concatenate([q_ref[r : r + 1, :] for r in range(RANK)], axis=1)
    for z in range(o_ref.shape[0]):
        o_ref[z] = flat


def share(
    far_grad_ref, far_res_ref, far_words_ref, far_bits_ref, far_ref, grad_ref, res_ref, words_ref, bits_ref, o_ref, sems
):
    theirs = pl.multiple_of((1 - lax.axis_index("c")) * HALF, HALF)
    words = pltpu.make_async_copy(far_words_ref.at[:, pl.ds(theirs, HALF)], words_ref, sems.at[0, 2])
    copies = []
    for i in range(FF // SHARE):
        at = pl.ds(i * SHARE, SHARE)
        copies.append(
            [
                pltpu.make_async_copy(far_grad_ref.at[:, at], grad_ref.at[:, at], sems.at[i, 0]),
                pltpu.make_async_copy(far_res_ref.at[:, at], res_ref.at[:, at], sems.at[i, 1]),
            ]
        )
        for copy in copies[i]:
            copy.start()
    words.start()
    late_bits = pltpu.make_async_copy(far_bits_ref, bits_ref, sems.at[2, 2])
    late_bits.start()
    sent = []

    def send(start, size, sem):
        at = pl.ds(start, size)
        sent.append(pltpu.make_async_copy(o_ref.at[:, at], far_ref.at[:, at], sem))
        sent[-1].start()

    for i in range(FF // SHARE):
        at = pl.ds(i * SHARE, SHARE)
        for copy in copies[i]:
            copy.wait()
        merged = grad_ref[:, at].astype(F32) + res_ref[:, at].astype(F32)
        for k in range(4):
            o_ref[:, k * FF + i * SHARE : k * FF + i * SHARE + SHARE] = merged[k * 8 : k * 8 + 8]
            send(k * FF + i * SHARE, SHARE, sems.at[i, 3 + k])
    words.wait()
    late_bits.wait()
    bits = bits_ref[...].astype(F32)
    o_ref[:, 4 * FF + HALF :] = jnp.concatenate([bits[0:8], bits[8:16], jnp.zeros((8, 64), F32)], axis=1)
    o_ref[:, 4 * FF : 4 * FF + HALF] = words_ref[...].astype(F32)
    send(4 * FF, HALF + 128, sems.at[1, 2])
    for copy in sent:
        copy.wait()


def merged_of(other_ref, start, size):
    return jnp.concatenate([other_ref[:, pl.ds(k * FF + start, size)] for k in range(4)], axis=0)


def spread_factor(x_ref, o_ref):
    pieces = x_ref[:, 0, :]
    for half in range(2):
        rows = [pieces[:, r * 40 : r * 40 + 40] for r in range(half * 8, half * 8 + 8)]
        packed = jnp.concatenate(rows, axis=0).T
        for s in range(16):
            o_ref[s * 2 + half] = packed


def left_factor(grad_ref, res_ref, other_ref, factor_ref, bits_ref, o_ref):
    c = lax.axis_index("c")
    factor = jnp.concatenate(parts(factor_ref[...].reshape(1280, 128), 2), axis=1)
    owner = lax.broadcasted_iota(jnp.int32, (ROWS, 128), 1) % 16
    totals = [jnp.zeros((ROWS, 128), F32), jnp.zeros((ROWS, 128), F32)]
    for z in range(0, 16, 4):
        places = [slice(k * 1280, k * 1280 + 1280) for k in range(z, z + 4)]
        split = [parts(merged_of(other_ref, k * 1280, 1280), 2) for k in range(z, z + 4)]
        rows = [grad_ref[:, at] for at in places] + [res_ref[:, at] for at in places]
        rows += [high for high, _ in split] + [low for _, low in split]
        prod = jnp.dot(jnp.concatenate(rows, axis=0), factor, preferred_element_type=F32)
        prod = prod[:, 0:128] + prod[:, 128:256]
        for w in range(2):
            both = prod[w * 256 : w * 256 + 128] + prod[w * 256 + 128 : w * 256 + 256]
            for k in range(4):
                totals[w] = totals[w] + jnp.where(owner == z + k, both[k * 32 : k * 32 + 32], 0.0)
    rank = lax.broadcasted_iota(jnp.int32, (8, 128), 0)
    lane = lax.broadcasted_iota(jnp.int32, (8, 128), 1)
    fold = jnp.where(lane // 16 == rank, 1.0, 0.0).astype(F32)
    here = bits_ref[...].astype(F32)
    there = other_ref[:, 4 * FF + HALF :]
    bits = (
        jnp.where(c == 0, here[0:8], here[8:16]),
        jnp.where(c == 0, there[:, 0:32], there[:, 32:64]),
    )
    sent = jnp.zeros((8, 32), F32)
    for w in range(2):
        local = lax.dot_general(
            fold, totals[w], (((1,), (1,)), ((), ())), precision=lax.Precision.HIGHEST, preferred_element_type=F32
        )
        noise = bits[w] * 2.0 ** (-21) - 0.5
        sent = sent + (local + noise * WIDTH * jnp.abs(local)).astype(BF16).astype(F32)
    tile = jnp.concatenate([sent[r : r + 2] for r in range(0, 8, 2)], axis=1)
    for s in range(o_ref.shape[0]):
        o_ref[s] = tile


def add_left(x_ref, o_ref):
    halves = []
    for c in range(2):
        total = x_ref[c]
        for s in range(1, 16):
            total = total + x_ref[s * 2 + c]
        halves.append(total)
    both = jnp.concatenate(halves, axis=0)
    for z in range(o_ref.shape[0]):
        o_ref[z] = both


def add_and_repeat(x_ref, o_ref):
    total = x_ref[0]
    for s in range(1, x_ref.shape[0]):
        total = total + x_ref[s]
    for s in range(o_ref.shape[0]):
        o_ref[s] = total


def orthonormal(columns):
    left = [jnp.broadcast_to(columns[:, k : k + 1], (ROWS, 128)) for k in range(RANK)]
    lane = lax.broadcasted_iota(jnp.int32, (ROWS, 128), 1)
    basis = jnp.zeros((ROWS, 128), F32)
    for j in range(RANK):
        unit = left[j] * lax.rsqrt(jnp.sum(left[j] * left[j], axis=0, keepdims=True))
        basis = jnp.where(lane == j, unit, basis)
        for k in range(j + 1, RANK):
            left[k] = left[k] - jnp.sum(unit * left[k], axis=0, keepdims=True) * unit
    return basis


def right_columns(split, first, second, words):
    prod = jnp.dot(split, jnp.concatenate([first, second], axis=0), preferred_element_type=F32)
    local = prod[0:16] + prod[16:32] + prod[32:48]
    low = (words & 127).astype(F32) * (1.0 / 128.0)
    high = (words >> 7).astype(F32) * (1.0 / 64.0)
    noise = jnp.concatenate([low, high], axis=0) - 0.5
    return (local + noise * WIDTH * jnp.abs(local)).astype(BF16).astype(F32)


def right_factor(tiles_ref, grad_ref, res_ref, words_ref, other_ref, turned_ref, o_ref):
    total = tiles_ref[0]
    for s in range(1, tiles_ref.shape[0]):
        total = total + tiles_ref[s]
    rows = [total[c * 2 : c * 2 + 2, q * 32 : q * 32 + 32] for c in range(2) for q in range(4)]
    basis = orthonormal(jnp.concatenate(rows, axis=0).T)
    turned_ref[...] = basis[:, 0:RANK]
    split = jnp.concatenate(parts(basis.T[0:RANK], 3), axis=0)
    split = jnp.concatenate([split, split], axis=1)
    base = lax.axis_index("c") * HALF
    for i in range(HALF // STEP):
        at = pl.ds(pl.multiple_of(base + i * STEP, STEP), STEP)
        sent = right_columns(split, grad_ref[:, at], res_ref[:, at], words_ref[:, at])
        high, low = parts(merged_of(other_ref, pl.multiple_of(base + i * STEP, STEP), STEP), 2)
        words = other_ref[:, 4 * FF + i * STEP : 4 * FF + i * STEP + STEP].astype(jnp.int32)
        sent = sent + right_columns(split, high, low, words)
        for t in range(STEP // BLOCK):
            o_ref[i * (STEP // BLOCK) + t] = sent[:, t * BLOCK : t * BLOCK + BLOCK]


def new_columns(side, turned_ref, grad_ref, res_ref, total_ref, o_ref, made_ref, sems):
    high, low = parts(turned_ref[...] * (1.0 / WORLD), 2)
    left = jnp.concatenate([high, low, high], axis=1)
    copies = []
    for i in range(HALF // STEP):
        at = pl.ds(pl.multiple_of(side * HALF + i * STEP, STEP), STEP)
        here = pl.ds(i * STEP, STEP)
        blocks = [total_ref[t] for t in range(i * STEP // BLOCK, (i + 1) * STEP // BLOCK)]
        th, tl = parts(jnp.concatenate(blocks, axis=1), 2)
        right = jnp.concatenate([th, th, tl], axis=0)
        approx = jnp.dot(left, right, preferred_element_type=F32)
        merged = grad_ref[:, at].astype(F32) + res_ref[:, at].astype(F32)
        made_ref[:, here] = (merged - approx).astype(BF16)
        copy = pltpu.make_async_copy(made_ref.at[:, here], o_ref.at[:, at], sems.at[i])
        copy.start()
        copies.append(copy)
    return copies


def update_first(turned_ref, grad_ref, res_ref, own_ref, o_ref, made_ref, sems):
    for copy in new_columns(lax.axis_index("c"), turned_ref, grad_ref, res_ref, own_ref, o_ref, made_ref, sems):
        copy.wait()


def update_second(
    turned_ref, grad_ref, res_ref, own_ref, rest_ref, done_ref, far_q_ref, o_ref, made_ref, sems, q_ref, q_sem
):
    c = lax.axis_index("c")
    device = ((lax.axis_index("zh") * 2 + lax.axis_index("zl")) * 16 + lax.axis_index("s")) * 2 + c
    block, offset = device // 16, (device % 16) * 40
    t = block % 16
    mine = jnp.where(block // 16 == c, own_ref[t], rest_ref[t])
    mine = pltpu.roll(mine, (BLOCK - offset) % BLOCK, 1)
    q_ref[...] = mine[:, 0:40] * WORLD ** (-0.5)
    copy_q = pltpu.make_async_copy(q_ref, far_q_ref, q_sem)
    copy_q.start()
    copies = new_columns(1 - c, turned_ref, grad_ref, res_ref, rest_ref, o_ref, made_ref, sems)
    copy_q.wait()
    for copy in copies:
        copy.wait()


def exchange(blocks, axis):
    return lax.all_to_all(blocks, axis, 0, 0, tiled=True)


def shards(gradient, residual, q_prev, p_bits, q_bits):
    z, plane, group = ("zh", "zl"), ("s", "c"), ("zl", "s")
    grad, res = gradient[0], residual[0]
    p_words, q_words = p_bits[0].T, q_bits[0].T
    swap = [(0, 1), (1, 0)]
    whole = pl.BlockSpec(memory_space=pltpu.VMEM)
    far = pl.BlockSpec(memory_space=pl.ANY)

    with jax.named_scope("share"):
        mine = call(
            share,
            jax.ShapeDtypeStruct((8, 4 * FF + HALF + 128), F32),
            limit=56 * 1024 * 1024,
            in_specs=[far] * 4,
            out_specs=far,
            scratch_shapes=[
                pltpu.VMEM((ROWS, FF), BF16),
                pltpu.VMEM((ROWS, FF), BF16),
                pltpu.VMEM((8, HALF), jnp.int32),
                pltpu.VMEM((RANK, ROWS), jnp.int32),
                pltpu.VMEM((8, 4 * FF + HALF + 128), F32),
                pltpu.SemaphoreType.DMA((FF // SHARE, 7)),
            ],
        )(grad, res, q_words, p_words)
        other = lax.ppermute(mine, "c", swap)
    with jax.named_scope("gather_q_prev"):
        pieces = call(pack_factor, jax.ShapeDtypeStruct((16, 1, 640), F32), in_specs=[whole], out_specs=whole)(q_prev.T)
        pieces = exchange(pieces, z)
        spread = call(
            spread_factor,
            jax.ShapeDtypeStruct((32, 40, 128), F32),
            in_specs=[whole],
            out_specs=whole,
            cost_estimate=pl.CostEstimate(flops=10**11, bytes_accessed=10**8, transcendentals=0),
        )(pieces)
        factor = exchange(spread, plane)
    with jax.named_scope("left_factor"):
        tile = call(left_factor, jax.ShapeDtypeStruct((32, 2, 128), F32), in_specs=[whole] * 5, out_specs=whole)(
            grad, res, other, factor, p_words
        )
        tile = exchange(tile, plane)
        tile = call(add_left, jax.ShapeDtypeStruct((16, 4, 128), F32), in_specs=[whole], out_specs=whole)(tile)
        tile = exchange(tile, z)
    steps = HALF // STEP
    with jax.named_scope("right_factor"):
        turned, summed = call(
            right_factor,
            (jax.ShapeDtypeStruct((32, 16), F32), jax.ShapeDtypeStruct((16, 16, BLOCK), F32)),
            in_specs=[whole] * 5,
            out_specs=(whole, whole),
        )(tile, grad, res, q_words, other)
        summed = summed.reshape(32, 8, BLOCK)
        summed = exchange(summed, group)
        summed = call(add_and_repeat, jax.ShapeDtypeStruct((8, 8, BLOCK), F32), in_specs=[whole], out_specs=whole)(summed)
        summed = exchange(summed, "zh")
        summed = call(add_and_repeat, jax.ShapeDtypeStruct((32, 8, BLOCK), F32), in_specs=[whole], out_specs=whole)(summed)
        total = exchange(summed, group).reshape(16, 16, BLOCK)
        rest = lax.ppermute(total, "c", swap)
    with jax.named_scope("update"):
        done = jax.ShapeDtypeStruct((ROWS, FF), BF16)
        room = [pltpu.VMEM((ROWS, HALF), BF16), pltpu.SemaphoreType.DMA((steps,))]
        updated = call(
            update_first, done, in_specs=[whole] * 4, out_specs=far, scratch_shapes=room
        )(turned, grad, res, total)
        q_next, updated = call(
            update_second,
            (jax.ShapeDtypeStruct((16, 40), F32), done),
            in_specs=[whole] * 5 + [far],
            out_specs=(far, far),
            scratch_shapes=room + [pltpu.VMEM((16, 40), F32), pltpu.SemaphoreType.DMA],
            input_output_aliases={5: 1},
        )(turned, grad, res, total, rest, updated)
    return (q_next.T, updated[None])


def solution(mesh):
    every = ("zh", "zl", "s", "c")
    split = Mesh(mesh.devices.reshape(8, 2, 16, 2), every)
    row, block = P(every, None), P(every, None, None)
    return jax.shard_map(
        shards,
        mesh=split,
        in_specs=(block, block, row, block, block),
        out_specs=(row, block),
        check_vma=False,
    )
```

```python
import functools

import jax
import jax.numpy as jnp
from jax import lax
from jax.experimental import pallas as pl
from jax.experimental.pallas import tpu as pltpu
from jax.sharding import Mesh, PartitionSpec as P

FF = 20480
RANK = 16
ROWS = 32
WORLD = 512
HALF = FF // 2
BLOCK = 640
STEP = 2560
SHARES = ((0, 5120), (5120, 6144), (11264, 6144), (17408, 3072))
WIDTH = 0.25
SHORT = [[0, 2, 4, 6, 9, 11, 13, 15], [1, 3, 5, 7, 8, 10, 12, 14]]
F32 = jnp.float32
BF16 = jnp.bfloat16
VMEM_LIMIT = 16 * 1024 * 1024


def call(body, out_shape, limit=VMEM_LIMIT, **kw):
    return pl.pallas_call(
        body,
        out_shape=out_shape,
        compiler_params=pltpu.CompilerParams(vmem_limit_bytes=limit),
        **kw,
    )


def parts(x, n):
    out = []
    for _ in range(n):
        p = x.astype(BF16)
        out.append(p)
        x = x - p.astype(F32)
    return out


def pack_factor(q_ref, o_ref):
    flat = jnp.concatenate([q_ref[r : r + 1, :] for r in range(RANK)], axis=1)
    for z in range(o_ref.shape[0]):
        o_ref[z] = flat


def share(
    far_grad_ref, far_res_ref, far_words_ref, far_bits_ref, far_ref, grad_ref, res_ref, words_ref, bits_ref, o_ref, sems
):
    theirs = pl.multiple_of((1 - lax.axis_index("c")) * HALF, HALF)
    words = pltpu.make_async_copy(far_words_ref.at[:, pl.ds(theirs, HALF)], words_ref, sems.at[0, 2])
    late_bits = pltpu.make_async_copy(far_bits_ref, bits_ref, sems.at[2, 2])
    words.start()
    late_bits.start()
    copies = []
    for i, (start, size) in enumerate(SHARES):
        at = pl.ds(start, size)
        copies.append(
            [
                pltpu.make_async_copy(far_grad_ref.at[:, at], grad_ref.at[:, at], sems.at[i, 0]),
                pltpu.make_async_copy(far_res_ref.at[:, at], res_ref.at[:, at], sems.at[i, 1]),
            ]
        )
        for copy in copies[i]:
            copy.start()
    sent = []

    def send(start, size, sem):
        at = pl.ds(start, size)
        sent.append(pltpu.make_async_copy(o_ref.at[:, at], far_ref.at[:, at], sem))
        sent[-1].start()

    words.wait()
    late_bits.wait()
    o_ref[:, 4 * FF : 4 * FF + HALF] = words_ref[...].astype(F32)
    bits = bits_ref[...].astype(F32)
    o_ref[:, 4 * FF + HALF :] = jnp.concatenate([bits[0:8], bits[8:16], jnp.zeros((8, 64), F32)], axis=1)
    send(4 * FF, HALF + 128, sems.at[1, 2])
    for i, (start, size) in enumerate(SHARES):
        at = pl.ds(start, size)
        for copy in copies[i]:
            copy.wait()
        merged = grad_ref[:, at].astype(F32) + res_ref[:, at].astype(F32)
        for k in range(4):
            o_ref[:, k * FF + start : k * FF + start + size] = merged[k * 8 : k * 8 + 8]
            send(k * FF + start, size, sems.at[i, 3 + k])
    for copy in sent:
        copy.wait()


def merged_of(other_ref, start, size):
    return jnp.concatenate([other_ref[:, pl.ds(k * FF + start, size)] for k in range(4)], axis=0)


def spread_factor(x_ref, o_ref):
    pieces = x_ref[:, 0, :]
    for half in range(2):
        rows = [pieces[:, r * 40 : r * 40 + 40] for r in range(half * 8, half * 8 + 8)]
        packed = jnp.concatenate(rows, axis=0).T
        for s in range(16):
            o_ref[s * 2 + half] = packed


def left_factor(grad_ref, res_ref, other_ref, factor_ref, bits_ref, o_ref):
    c = lax.axis_index("c")
    factor = jnp.concatenate(parts(factor_ref[...].reshape(1280, 128), 2), axis=1)
    owner = lax.broadcasted_iota(jnp.int32, (ROWS, 128), 1) % 16
    totals = [jnp.zeros((ROWS, 128), F32), jnp.zeros((ROWS, 128), F32)]
    for z in range(0, 16, 4):
        places = [slice(k * 1280, k * 1280 + 1280) for k in range(z, z + 4)]
        split = [parts(merged_of(other_ref, k * 1280, 1280), 2) for k in range(z, z + 4)]
        rows = [grad_ref[:, at] for at in places] + [res_ref[:, at] for at in places]
        rows += [high for high, _ in split] + [low for _, low in split]
        prod = jnp.dot(jnp.concatenate(rows, axis=0), factor, preferred_element_type=F32)
        prod = prod[:, 0:128] + prod[:, 128:256]
        for w in range(2):
            both = prod[w * 256 : w * 256 + 128] + prod[w * 256 + 128 : w * 256 + 256]
            for k in range(4):
                totals[w] = totals[w] + jnp.where(owner == z + k, both[k * 32 : k * 32 + 32], 0.0)
    rank = lax.broadcasted_iota(jnp.int32, (8, 128), 0)
    lane = lax.broadcasted_iota(jnp.int32, (8, 128), 1)
    fold = jnp.where(lane // 16 == rank, 1.0, 0.0).astype(F32)
    here = bits_ref[...].astype(F32)
    there = other_ref[:, 4 * FF + HALF :]
    bits = (
        jnp.where(c == 0, here[0:8], here[8:16]),
        jnp.where(c == 0, there[:, 0:32], there[:, 32:64]),
    )
    sent = jnp.zeros((8, 32), F32)
    for w in range(2):
        local = lax.dot_general(
            fold, totals[w], (((1,), (1,)), ((), ())), precision=lax.Precision.HIGHEST, preferred_element_type=F32
        )
        noise = bits[w] * 2.0 ** (-21) - 0.5
        sent = sent + (local + noise * WIDTH * jnp.abs(local)).astype(BF16).astype(F32)
    tile = jnp.concatenate([sent[r : r + 2] for r in range(0, 8, 2)], axis=1)
    for s in range(o_ref.shape[0]):
        o_ref[s] = tile


def add_left(x_ref, o_ref):
    halves = []
    for c in range(2):
        total = x_ref[c]
        for s in range(1, 16):
            total = total + x_ref[s * 2 + c]
        halves.append(total)
    both = jnp.concatenate(halves, axis=0)
    for z in range(o_ref.shape[0]):
        o_ref[z] = both


def add_and_repeat(x_ref, o_ref):
    total = x_ref[0]
    for s in range(1, x_ref.shape[0]):
        total = total + x_ref[s]
    for s in range(o_ref.shape[0]):
        o_ref[s] = total


def orthonormal(columns):
    left = [jnp.broadcast_to(columns[:, k : k + 1], (ROWS, 128)) for k in range(RANK)]
    lane = lax.broadcasted_iota(jnp.int32, (ROWS, 128), 1)
    basis = jnp.zeros((ROWS, 128), F32)
    for j in range(RANK):
        unit = left[j] * lax.rsqrt(jnp.sum(left[j] * left[j], axis=0, keepdims=True))
        basis = jnp.where(lane == j, unit, basis)
        for k in range(j + 1, RANK):
            left[k] = left[k] - jnp.sum(unit * left[k], axis=0, keepdims=True) * unit
    return basis


def right_columns(split, first, second, words):
    prod = jnp.dot(split, jnp.concatenate([first, second], axis=0), preferred_element_type=F32)
    local = prod[0:16] + prod[16:32] + prod[32:48]
    low = (words & 127).astype(F32) * (1.0 / 128.0)
    high = (words >> 7).astype(F32) * (1.0 / 64.0)
    noise = jnp.concatenate([low, high], axis=0) - 0.5
    return (local + noise * WIDTH * jnp.abs(local)).astype(BF16).astype(F32)


def right_factor(tiles_ref, grad_ref, res_ref, words_ref, other_ref, turned_ref, o_ref):
    total = tiles_ref[0]
    for s in range(1, tiles_ref.shape[0]):
        total = total + tiles_ref[s]
    rows = [total[c * 2 : c * 2 + 2, q * 32 : q * 32 + 32] for c in range(2) for q in range(4)]
    basis = orthonormal(jnp.concatenate(rows, axis=0).T)
    turned_ref[...] = basis[:, 0:RANK]
    split = jnp.concatenate(parts(basis.T[0:RANK], 3), axis=0)
    split = jnp.concatenate([split, split], axis=1)
    base = lax.axis_index("c") * HALF
    turn = lax.axis_index("zh") // 4 * 8
    for i in range(HALF // STEP):
        at = pl.ds(pl.multiple_of(base + i * STEP, STEP), STEP)
        sent = right_columns(split, grad_ref[:, at], res_ref[:, at], words_ref[:, at])
        high, low = parts(merged_of(other_ref, pl.multiple_of(base + i * STEP, STEP), STEP), 2)
        words = other_ref[:, 4 * FF + i * STEP : 4 * FF + i * STEP + STEP].astype(jnp.int32)
        sent = sent + right_columns(split, high, low, words)
        for t in range(STEP // BLOCK):
            o_ref[(i * (STEP // BLOCK) + t + turn) % 16] = sent[:, t * BLOCK : t * BLOCK + BLOCK]


def new_columns(side, turned_ref, grad_ref, res_ref, total_ref, o_ref, made_ref, sems):
    high, low = parts(turned_ref[...] * (1.0 / WORLD), 2)
    left = jnp.concatenate([high, low, high], axis=1)
    turn = lax.axis_index("zh") // 4 * 8
    copies = []
    for i in range(HALF // STEP):
        at = pl.ds(pl.multiple_of(side * HALF + i * STEP, STEP), STEP)
        here = pl.ds(i * STEP, STEP)
        blocks = [total_ref[(t + turn) % 16] for t in range(i * STEP // BLOCK, (i + 1) * STEP // BLOCK)]
        th, tl = parts(jnp.concatenate(blocks, axis=1), 2)
        right = jnp.concatenate([th, th, tl], axis=0)
        approx = jnp.dot(left, right, preferred_element_type=F32)
        merged = grad_ref[:, at].astype(F32) + res_ref[:, at].astype(F32)
        made_ref[:, here] = (merged - approx).astype(BF16)
        copy = pltpu.make_async_copy(made_ref.at[:, here], o_ref.at[:, at], sems.at[i])
        copy.start()
        copies.append(copy)
    return copies


def update_first(turned_ref, grad_ref, res_ref, own_ref, o_ref, made_ref, sems):
    for copy in new_columns(lax.axis_index("c"), turned_ref, grad_ref, res_ref, own_ref, o_ref, made_ref, sems):
        copy.wait()


def update_second(
    turned_ref, grad_ref, res_ref, own_ref, rest_ref, done_ref, far_q_ref, o_ref, made_ref, sems, q_ref, q_sem
):
    c = lax.axis_index("c")
    device = ((lax.axis_index("zh") * 2 + lax.axis_index("zl")) * 16 + lax.axis_index("s")) * 2 + c
    block, offset = device // 16, (device % 16) * 40
    t = (block + lax.axis_index("zh") // 4 * 8) % 16
    mine = jnp.where(block // 16 == c, own_ref[t], rest_ref[t])
    mine = pltpu.roll(mine, (BLOCK - offset) % BLOCK, 1)
    q_ref[...] = mine[:, 0:40] * WORLD ** (-0.5)
    copy_q = pltpu.make_async_copy(q_ref, far_q_ref, q_sem)
    copy_q.start()
    copies = new_columns(1 - c, turned_ref, grad_ref, res_ref, rest_ref, o_ref, made_ref, sems)
    copy_q.wait()
    for copy in copies:
        copy.wait()


def exchange(blocks, axis, groups=None):
    return lax.all_to_all(blocks, axis, 0, 0, tiled=True, axis_index_groups=groups)


def shards(gradient, residual, q_prev, p_bits, q_bits):
    z, plane, group = ("zh", "zl"), ("s", "c"), ("zl", "s")
    grad, res = gradient[0], residual[0]
    p_words, q_words = p_bits[0].T, q_bits[0].T
    swap = [(0, 1), (1, 0)]
    whole = pl.BlockSpec(memory_space=pltpu.VMEM)
    far = pl.BlockSpec(memory_space=pl.ANY)

    with jax.named_scope("share"):
        mine = call(
            share,
            jax.ShapeDtypeStruct((8, 4 * FF + HALF + 128), F32),
            limit=56 * 1024 * 1024,
            in_specs=[far] * 4,
            out_specs=far,
            scratch_shapes=[
                pltpu.VMEM((ROWS, FF), BF16),
                pltpu.VMEM((ROWS, FF), BF16),
                pltpu.VMEM((8, HALF), jnp.int32),
                pltpu.VMEM((RANK, ROWS), jnp.int32),
                pltpu.VMEM((8, 4 * FF + HALF + 128), F32),
                pltpu.SemaphoreType.DMA((len(SHARES), 7)),
            ],
        )(grad, res, q_words, p_words)
        other = lax.ppermute(mine, "c", swap)
    with jax.named_scope("gather_q_prev"):
        pieces = call(pack_factor, jax.ShapeDtypeStruct((16, 1, 640), F32), in_specs=[whole], out_specs=whole)(q_prev.T)
        pieces = exchange(pieces, z)
        spread = call(
            spread_factor,
            jax.ShapeDtypeStruct((32, 40, 128), F32),
            in_specs=[whole],
            out_specs=whole,
            cost_estimate=pl.CostEstimate(flops=10**11, bytes_accessed=10**8, transcendentals=0),
        )(pieces)
        factor = exchange(spread, plane)
    with jax.named_scope("left_factor"):
        tile = call(left_factor, jax.ShapeDtypeStruct((32, 2, 128), F32), in_specs=[whole] * 5, out_specs=whole)(
            grad, res, other, factor, p_words
        )
        tile = exchange(tile, plane)
        tile = call(add_left, jax.ShapeDtypeStruct((16, 4, 128), F32), in_specs=[whole], out_specs=whole)(tile)
        tile = exchange(tile, z)
    steps = HALF // STEP
    with jax.named_scope("right_factor"):
        turned, summed = call(
            right_factor,
            (jax.ShapeDtypeStruct((32, 16), F32), jax.ShapeDtypeStruct((16, 16, BLOCK), F32)),
            in_specs=[whole] * 5,
            out_specs=(whole, whole),
        )(tile, grad, res, q_words, other)
        summed = summed.reshape(32, 8, BLOCK)
        summed = exchange(summed, group)
        summed = call(add_and_repeat, jax.ShapeDtypeStruct((8, 8, BLOCK), F32), in_specs=[whole], out_specs=whole)(summed)
        summed = exchange(summed, z, SHORT)
        summed = call(add_and_repeat, jax.ShapeDtypeStruct((32, 8, BLOCK), F32), in_specs=[whole], out_specs=whole)(summed)
        total = exchange(summed, group).reshape(16, 16, BLOCK)
        rest = lax.ppermute(total, "c", swap)
    with jax.named_scope("update"):
        done = jax.ShapeDtypeStruct((ROWS, FF), BF16)
        room = [pltpu.VMEM((ROWS, HALF), BF16), pltpu.SemaphoreType.DMA((steps,))]
        updated = call(
            update_first, done, in_specs=[whole] * 4, out_specs=far, scratch_shapes=room
        )(turned, grad, res, total)
        q_next, updated = call(
            update_second,
            (jax.ShapeDtypeStruct((16, 40), F32), done),
            in_specs=[whole] * 5 + [far],
            out_specs=(far, far),
            scratch_shapes=room + [pltpu.VMEM((16, 40), F32), pltpu.SemaphoreType.DMA],
            input_output_aliases={5: 1},
        )(turned, grad, res, total, rest, updated)
    return (q_next.T, updated[None])


def solution(mesh):
    every = ("zh", "zl", "s", "c")
    split = Mesh(mesh.devices.reshape(8, 2, 16, 2), every)
    row, block = P(every, None), P(every, None, None)
    return jax.shard_map(
        shards,
        mesh=split,
        in_specs=(block, block, row, block, block),
        out_specs=(row, block),
        check_vma=False,
    )
```

```python
import functools

import jax
import jax.numpy as jnp
from jax import lax
from jax.experimental import pallas as pl
from jax.experimental.pallas import tpu as pltpu
from jax.sharding import Mesh, PartitionSpec as P

FF = 20480
RANK = 16
ROWS = 32
WORLD = 512
HALF = FF // 2
BLOCK = 640
STEP = 2560
SHARE = 5120
WIDTH = 0.25
F32 = jnp.float32
BF16 = jnp.bfloat16
VMEM_LIMIT = 16 * 1024 * 1024


def call(body, out_shape, limit=VMEM_LIMIT, **kw):
    return pl.pallas_call(
        body,
        out_shape=out_shape,
        compiler_params=pltpu.CompilerParams(vmem_limit_bytes=limit),
        **kw,
    )


def parts(x, n):
    out = []
    for _ in range(n):
        p = x.astype(BF16)
        out.append(p)
        x = x - p.astype(F32)
    return out


def pack_factor(q_ref, o_ref):
    flat = jnp.concatenate([q_ref[r : r + 1, :] for r in range(RANK)], axis=1)
    for z in range(o_ref.shape[0]):
        o_ref[z] = flat


def share(
    far_grad_ref, far_res_ref, far_words_ref, far_bits_ref, far_ref, grad_ref, res_ref, words_ref, bits_ref, o_ref, sems
):
    theirs = pl.multiple_of((1 - lax.axis_index("c")) * HALF, HALF)
    words = pltpu.make_async_copy(far_words_ref.at[:, pl.ds(theirs, HALF)], words_ref, sems.at[0, 2])
    copies = []
    for i in range(FF // SHARE):
        at = pl.ds(i * SHARE, SHARE)
        copies.append(
            [
                pltpu.make_async_copy(far_grad_ref.at[:, at], grad_ref.at[:, at], sems.at[i, 0]),
                pltpu.make_async_copy(far_res_ref.at[:, at], res_ref.at[:, at], sems.at[i, 1]),
            ]
        )
        for copy in copies[i]:
            copy.start()
    words.start()
    late_bits = pltpu.make_async_copy(far_bits_ref, bits_ref, sems.at[2, 2])
    late_bits.start()
    sent = []

    def send(start, size, sem):
        at = pl.ds(start, size)
        sent.append(pltpu.make_async_copy(o_ref.at[:, at], far_ref.at[:, at], sem))
        sent[-1].start()

    for i in range(FF // SHARE):
        at = pl.ds(i * SHARE, SHARE)
        for copy in copies[i]:
            copy.wait()
        merged = grad_ref[:, at].astype(F32) + res_ref[:, at].astype(F32)
        for k in range(4):
            o_ref[:, k * FF + i * SHARE : k * FF + i * SHARE + SHARE] = merged[k * 8 : k * 8 + 8]
            send(k * FF + i * SHARE, SHARE, sems.at[i, 3 + k])
    words.wait()
    late_bits.wait()
    bits = bits_ref[...].astype(F32)
    o_ref[:, 4 * FF + HALF :] = jnp.concatenate([bits[0:8], bits[8:16], jnp.zeros((8, 64), F32)], axis=1)
    o_ref[:, 4 * FF : 4 * FF + HALF] = words_ref[...].astype(F32)
    send(4 * FF, HALF + 128, sems.at[1, 2])
    for copy in sent:
        copy.wait()


def merged_of(other_ref, start, size):
    return jnp.concatenate([other_ref[:, pl.ds(k * FF + start, size)] for k in range(4)], axis=0)


def spread_factor(x_ref, o_ref):
    pieces = x_ref[:, 0, :]
    for half in range(2):
        rows = [pieces[:, r * 40 : r * 40 + 40] for r in range(half * 8, half * 8 + 8)]
        packed = jnp.concatenate(rows, axis=0).T
        for s in range(16):
            o_ref[half * 16 + s] = packed


def left_factor(grad_ref, res_ref, other_ref, factor_ref, bits_ref, o_ref):
    c = lax.axis_index("c")
    whole = jnp.concatenate([factor_ref[k * 16 + s] for s in range(16) for k in range(2)], axis=0)
    factor = jnp.concatenate(parts(whole, 2), axis=1)
    owner = lax.broadcasted_iota(jnp.int32, (ROWS, 128), 1) % 16
    totals = [jnp.zeros((ROWS, 128), F32), jnp.zeros((ROWS, 128), F32)]
    for z in range(0, 16, 2):
        places = [slice(k * 1280, k * 1280 + 1280) for k in range(z, z + 2)]
        split = [parts(merged_of(other_ref, k * 1280, 1280), 2) for k in range(z, z + 2)]
        rows = [grad_ref[:, at] for at in places] + [res_ref[:, at] for at in places]
        rows += [high for high, _ in split] + [low for _, low in split]
        prod = jnp.dot(jnp.concatenate(rows, axis=0), factor, preferred_element_type=F32)
        prod = prod[:, 0:128] + prod[:, 128:256]
        for w in range(2):
            both = prod[w * 128 : w * 128 + 64] + prod[w * 128 + 64 : w * 128 + 128]
            for k in range(2):
                totals[w] = totals[w] + jnp.where(owner == z + k, both[k * 32 : k * 32 + 32], 0.0)
    rank = lax.broadcasted_iota(jnp.int32, (8, 128), 0)
    lane = lax.broadcasted_iota(jnp.int32, (8, 128), 1)
    fold = jnp.where(lane // 16 == rank, 1.0, 0.0).astype(F32)
    here = bits_ref[...].astype(F32)
    there = other_ref[:, 4 * FF + HALF :]
    bits = (
        jnp.where(c == 0, here[0:8], here[8:16]),
        jnp.where(c == 0, there[:, 0:32], there[:, 32:64]),
    )
    sent = jnp.zeros((8, 32), F32)
    for w in range(2):
        local = lax.dot_general(
            fold, totals[w], (((1,), (1,)), ((), ())), precision=lax.Precision.HIGHEST, preferred_element_type=F32
        )
        noise = bits[w] * 2.0 ** (-21) - 0.5
        sent = sent + (local + noise * WIDTH * jnp.abs(local)).astype(BF16).astype(F32)
    tile = jnp.concatenate([sent[r : r + 2] for r in range(0, 8, 2)], axis=1)
    for s in range(o_ref.shape[0]):
        o_ref[s] = tile


def add_left(x_ref, o_ref):
    halves = []
    for c in range(2):
        total = x_ref[c * 16]
        for s in range(1, 16):
            total = total + x_ref[c * 16 + s]
        halves.append(total)
    both = jnp.concatenate(halves, axis=0)
    for z in range(o_ref.shape[0]):
        o_ref[z] = both


def add_and_repeat(x_ref, o_ref):
    total = x_ref[0]
    for s in range(1, x_ref.shape[0]):
        total = total + x_ref[s]
    for s in range(o_ref.shape[0]):
        o_ref[s] = total


def orthonormal(columns):
    left = [jnp.broadcast_to(columns[:, k : k + 1], (ROWS, 128)) for k in range(RANK)]
    lane = lax.broadcasted_iota(jnp.int32, (ROWS, 128), 1)
    basis = jnp.zeros((ROWS, 128), F32)
    for j in range(RANK):
        unit = left[j] * lax.rsqrt(jnp.sum(left[j] * left[j], axis=0, keepdims=True))
        basis = jnp.where(lane == j, unit, basis)
        for k in range(j + 1, RANK):
            left[k] = left[k] - jnp.sum(unit * left[k], axis=0, keepdims=True) * unit
    return basis


def right_columns(split, first, second, words):
    prod = jnp.dot(split, jnp.concatenate([first, second], axis=0), preferred_element_type=F32)
    local = prod[0:16] + prod[16:32] + prod[32:48]
    low = (words & 127).astype(F32) * (1.0 / 128.0)
    high = (words >> 7).astype(F32) * (1.0 / 64.0)
    noise = jnp.concatenate([low, high], axis=0) - 0.5
    return (local + noise * WIDTH * jnp.abs(local)).astype(BF16).astype(F32)


def right_factor(tiles_ref, grad_ref, res_ref, words_ref, other_ref, turned_ref, o_ref):
    total = tiles_ref[0]
    for s in range(1, tiles_ref.shape[0]):
        total = total + tiles_ref[s]
    rows = [total[c * 2 : c * 2 + 2, q * 32 : q * 32 + 32] for c in range(2) for q in range(4)]
    basis = orthonormal(jnp.concatenate(rows, axis=0).T)
    turned_ref[...] = basis[:, 0:RANK]
    split = jnp.concatenate(parts(basis.T[0:RANK], 3), axis=0)
    split = jnp.concatenate([split, split], axis=1)
    base = lax.axis_index("c") * HALF
    for i in range(HALF // STEP):
        at = pl.ds(pl.multiple_of(base + i * STEP, STEP), STEP)
        sent = right_columns(split, grad_ref[:, at], res_ref[:, at], words_ref[:, at])
        high, low = parts(merged_of(other_ref, pl.multiple_of(base + i * STEP, STEP), STEP), 2)
        words = other_ref[:, 4 * FF + i * STEP : 4 * FF + i * STEP + STEP].astype(jnp.int32)
        sent = sent + right_columns(split, high, low, words)
        for t in range(STEP // BLOCK):
            o_ref[i * (STEP // BLOCK) + t] = sent[:, t * BLOCK : t * BLOCK + BLOCK]


def new_columns(side, turned_ref, grad_ref, res_ref, total_ref, o_ref, made_ref, sems):
    high, low = parts(turned_ref[...] * (1.0 / WORLD), 2)
    left = jnp.concatenate([high, low, high], axis=1)
    copies = []
    for i in range(HALF // STEP):
        at = pl.ds(pl.multiple_of(side * HALF + i * STEP, STEP), STEP)
        here = pl.ds(i * STEP, STEP)
        blocks = [total_ref[t] for t in range(i * STEP // BLOCK, (i + 1) * STEP // BLOCK)]
        th, tl = parts(jnp.concatenate(blocks, axis=1), 2)
        right = jnp.concatenate([th, th, tl], axis=0)
        approx = jnp.dot(left, right, preferred_element_type=F32)
        merged = grad_ref[:, at].astype(F32) + res_ref[:, at].astype(F32)
        made_ref[:, here] = (merged - approx).astype(BF16)
        copy = pltpu.make_async_copy(made_ref.at[:, here], o_ref.at[:, at], sems.at[i])
        copy.start()
        copies.append(copy)
    return copies


def update_first(turned_ref, grad_ref, res_ref, own_ref, o_ref, made_ref, sems):
    for copy in new_columns(lax.axis_index("c"), turned_ref, grad_ref, res_ref, own_ref, o_ref, made_ref, sems):
        copy.wait()


def update_second(
    turned_ref, grad_ref, res_ref, own_ref, rest_ref, done_ref, far_q_ref, o_ref, made_ref, sems, q_ref, q_sem
):
    c = lax.axis_index("c")
    device = ((lax.axis_index("zh") * 2 + lax.axis_index("zl")) * 16 + lax.axis_index("s")) * 2 + c
    block, offset = device // 16, (device % 16) * 40
    t = block % 16
    mine = jnp.where(block // 16 == c, own_ref[t], rest_ref[t])
    mine = pltpu.roll(mine, (BLOCK - offset) % BLOCK, 1)
    q_ref[...] = mine[:, 0:40] * WORLD ** (-0.5)
    copy_q = pltpu.make_async_copy(q_ref, far_q_ref, q_sem)
    copy_q.start()
    copies = new_columns(1 - c, turned_ref, grad_ref, res_ref, rest_ref, o_ref, made_ref, sems)
    copy_q.wait()
    for copy in copies:
        copy.wait()


def exchange(blocks, axis):
    return lax.all_to_all(blocks, axis, 0, 0, tiled=True)


def shards(gradient, residual, q_prev, p_bits, q_bits):
    z, plane, group = ("zh", "zl"), ("c", "s"), ("zl", "s")
    grad, res = gradient[0], residual[0]
    p_words, q_words = p_bits[0].T, q_bits[0].T
    swap = [(0, 1), (1, 0)]
    whole = pl.BlockSpec(memory_space=pltpu.VMEM)
    far = pl.BlockSpec(memory_space=pl.ANY)

    with jax.named_scope("share"):
        mine = call(
            share,
            jax.ShapeDtypeStruct((8, 4 * FF + HALF + 128), F32),
            limit=56 * 1024 * 1024,
            in_specs=[far] * 4,
            out_specs=far,
            scratch_shapes=[
                pltpu.VMEM((ROWS, FF), BF16),
                pltpu.VMEM((ROWS, FF), BF16),
                pltpu.VMEM((8, HALF), jnp.int32),
                pltpu.VMEM((RANK, ROWS), jnp.int32),
                pltpu.VMEM((8, 4 * FF + HALF + 128), F32),
                pltpu.SemaphoreType.DMA((FF // SHARE, 7)),
            ],
        )(grad, res, q_words, p_words)
        other = lax.ppermute(mine, "c", swap)
    with jax.named_scope("gather_q_prev"):
        pieces = call(pack_factor, jax.ShapeDtypeStruct((16, 1, 640), F32), in_specs=[whole], out_specs=whole)(q_prev.T)
        pieces = exchange(pieces, z)
        spread = call(
            spread_factor,
            jax.ShapeDtypeStruct((32, 40, 128), F32),
            in_specs=[whole],
            out_specs=whole,
            cost_estimate=pl.CostEstimate(flops=10**11, bytes_accessed=10**8, transcendentals=0),
        )(pieces)
        factor = exchange(spread, plane)
    with jax.named_scope("left_factor"):
        tile = call(left_factor, jax.ShapeDtypeStruct((32, 2, 128), F32), in_specs=[whole] * 5, out_specs=whole)(
            grad, res, other, factor, p_words
        )
        tile = exchange(tile, plane)
        tile = call(add_left, jax.ShapeDtypeStruct((16, 4, 128), F32), in_specs=[whole], out_specs=whole)(tile)
        tile = exchange(tile, z)
    steps = HALF // STEP
    with jax.named_scope("right_factor"):
        turned, summed = call(
            right_factor,
            (jax.ShapeDtypeStruct((32, 16), F32), jax.ShapeDtypeStruct((16, 16, BLOCK), F32)),
            in_specs=[whole] * 5,
            out_specs=(whole, whole),
        )(tile, grad, res, q_words, other)
        summed = summed.reshape(32, 8, BLOCK)
        summed = exchange(summed, group)
        summed = call(add_and_repeat, jax.ShapeDtypeStruct((8, 8, BLOCK), F32), in_specs=[whole], out_specs=whole)(summed)
        summed = exchange(summed, "zh")
        summed = call(add_and_repeat, jax.ShapeDtypeStruct((32, 8, BLOCK), F32), in_specs=[whole], out_specs=whole)(summed)
        total = exchange(summed, group).reshape(16, 16, BLOCK)
        rest = lax.ppermute(total, "c", swap)
    with jax.named_scope("update"):
        done = jax.ShapeDtypeStruct((ROWS, FF), BF16)
        room = [pltpu.VMEM((ROWS, HALF), BF16), pltpu.SemaphoreType.DMA((steps,))]
        updated = call(
            update_first, done, in_specs=[whole] * 4, out_specs=far, scratch_shapes=room
        )(turned, grad, res, total)
        q_next, updated = call(
            update_second,
            (jax.ShapeDtypeStruct((16, 40), F32), done),
            in_specs=[whole] * 5 + [far],
            out_specs=(far, far),
            scratch_shapes=room + [pltpu.VMEM((16, 40), F32), pltpu.SemaphoreType.DMA],
            input_output_aliases={5: 1},
        )(turned, grad, res, total, rest, updated)
    return (q_next.T, updated[None])


def solution(mesh):
    every = ("zh", "zl", "s", "c")
    split = Mesh(mesh.devices.reshape(8, 2, 16, 2), every)
    row, block = P(every, None), P(every, None, None)
    return jax.shard_map(
        shards,
        mesh=split,
        in_specs=(block, block, row, block, block),
        out_specs=(row, block),
        check_vma=False,
    )
```
